256 devices in a mesh: pool: 32 (over x, y, core), tp: 8 (over z).
Axes of the slice: x: 4, y: 4, z: 8, core: 2. Of those that a mesh axis runs over, the one named last changes fastest.
Arguments:
- tokens: bfloat16 [2, 8192, 8192], P(None, 'pool', 'tp'), may hold values from -6 to 6
- query_weight: bfloat16 [8192, 4096], P('tp'), may hold values from -0.0625 to 0.0625
- down_weight: bfloat16 [512, 64, 8192], P('pool', None, 'tp'), may hold values from -0.0625 to 0.0625
- up_weight: bfloat16 [512, 64, 4096], P('pool', None, 'tp'), may hold values from -0.75 to 0.75
- requests: int32 [2, 32, 32], P(None, 'pool'), may hold values from 0 to 15
- row_slot_index: int32 [2, 32, 256], P(None, 'pool'), may hold values from 0 to 31, never falling along the last dimension, each value on 1 to 32 neighbouring positions
Outputs:
- queries: bfloat16 [2, 8192, 4096], P(None, 'pool', 'tp')
The draws below stay inside these ranges and needn't reach their ends.
Inputs may be any that keep to these rules, and one draw needn't show every extreme that they name: `requests`: slot s of every group names an adapter held by group s. `row_slot_index`: within one group and step the slots never fall from row to row; every slot is used by 1 to 32 rows, and one slot by exactly 32.
All inputs are finite; a program needn't handle non-finite values.
Results may differ from the reference program's by a relative error of at most 0.0049.
Values may be sent and summed in bfloat16 or wider, within the bound.
No kernel may reach another device: no remote copies, remote signals or barrier semaphores. Data moves between devices by JAX's collectives and lax.ppermute only.
A program may use at most 128 MiB of HBM per device.

```python
import math
from functools import partial
import jax
import jax.numpy as jnp
import numpy as np
from jax import lax

MODEL_WIDTH = 8192
QUERY_FEATURES = 4096
ADAPTER_RANK = 64
AD_GRP = 16
ROWS = 256
STEPS = 2
ADAPTER_TOTAL = 512
TOKENS = 8192
MOST = 32
N_POOL = 32


def place_ends(drawn, rng, least, largest):
    extent = drawn.shape
    spot = [jax.random.randint(jax.random.fold_in(rng, axis), (), 0, extent[axis]) for axis in range(len(extent))]
    drawn = drawn.at[tuple(spot)].set(least)
    longest = extent.index(max(extent))
    spot[longest] = (spot[longest] + 1) % extent[longest]
    return drawn.at[tuple(spot)].set(largest)


def levels(key, shape, cuts, low, top_value):
    loudness, own = 1.0, jax.random.fold_in(key, 6)
    for dim, parts in cuts:
        heights = jnp.exp(jax.random.uniform(jax.random.fold_in(own, dim), (parts,), jnp.float32, low / len(cuts), top_value / len(cuts)))
        loudness = loudness * jnp.repeat(heights, shape[dim] // parts).reshape([-1 if axis == dim else 1 for axis in range(len(shape))])
    return loudness


def length_profile(amount, total, limit, skew):
    weights = [(1 << 20) // math.isqrt(grade ** skew) + 1 for grade in range(2, amount + 1)]
    surplus, holding = total - limit - (amount - 1), [1] * (amount - 1)
    while surplus > 0:
        movable = [i for i in range(amount - 1) if holding[i] < limit]
        pool, budget = sum([weights[i] for i in movable]), surplus
        for i in movable:
            extra = min(limit - holding[i], max(1, budget * weights[i] // pool), surplus)
            holding[i] = holding[i] + extra
            surplus = surplus - extra
    return np.array([limit] + holding)


def ragged_sizes(key, count, total, limit, skew):
    if count == 2:
        one = jax.random.randint(key, (), max(1, total - limit), min(limit, total - 1) + 1)
        return jnp.stack([one, total - one])
    tallies = jnp.asarray(length_profile(count, total, limit, skew), jnp.int32)
    pairs = (count - 1) // 2
    donor, receiver = tallies[1:1 + 2 * pairs:2], tallies[2:2 + 2 * pairs:2]
    slack = jnp.minimum(donor - 1, limit - receiver)
    passed = jax.random.randint(jax.random.fold_in(key, 1), (pairs,), 0, 1 << 20) % (slack + 1)
    tallies = tallies.at[1:1 + 2 * pairs:2].set(donor - passed).at[2:2 + 2 * pairs:2].set(receiver + passed)
    return tallies[jax.random.permutation(jax.random.fold_in(key, 2), count)]


def gaussian(stream_key, dims, deviation, most, cuts=(), held_as=jnp.bfloat16):
    result = jax.random.normal(stream_key, dims, jnp.float32) * deviation
    if len(cuts) > 0:
        result = levels(stream_key, dims, cuts, -0.22, 0.18) * result
    return jnp.clip(result, min=-most, max=most).astype(held_as)


def setup_inputs(seed: int = 0) -> dict:
    keys = jax.random.split(jax.random.key(seed), 7)
    tokens = gaussian(keys[0], (STEPS, TOKENS, MODEL_WIDTH), 1.0, 6.0, ((1, 32), (2, 8)))
    query_weight = gaussian(keys[1], (MODEL_WIDTH, QUERY_FEATURES), MODEL_WIDTH ** -0.5, 0.0625, ((0, 8),))
    down_weight = gaussian(keys[2], (ADAPTER_TOTAL, ADAPTER_RANK, MODEL_WIDTH), MODEL_WIDTH ** -0.5, 0.0625, ((0, 32), (2, 8)))
    up_weight = gaussian(keys[3], (ADAPTER_TOTAL, ADAPTER_RANK, QUERY_FEATURES), ADAPTER_RANK ** -0.5, 0.75, ((0, 32), (2, 8)))
    requests = place_ends(jax.random.randint(keys[4], (STEPS, N_POOL, N_POOL), 0, AD_GRP), jax.random.fold_in(keys[4], 1), 0, AD_GRP - 1).astype(jnp.int32)
    row_slot_index = jax.vmap(lambda own: jnp.searchsorted(jnp.cumsum(ragged_sizes(own, N_POOL, ROWS, MOST, 2)), jnp.arange(ROWS), side="right"))(jax.random.split(keys[5], STEPS * N_POOL)).reshape((STEPS, N_POOL, ROWS)).astype(jnp.int32)
    return dict(tokens=tokens, query_weight=query_weight, down_weight=down_weight, up_weight=up_weight, requests=requests, row_slot_index=row_slot_index)


def grouped_delta(down_weight, up_weight, arguments):
    rows_x, wanted_pages, slot_list = arguments
    adapter_index = jnp.arange(N_POOL, dtype=jnp.int32) * AD_GRP + wanted_pages
    down_pages = down_weight[adapter_index].astype(jnp.float32)
    up_pages = up_weight[adapter_index].astype(jnp.float32)
    onehot = (slot_list[:, None] == jnp.arange(N_POOL, dtype=jnp.int32)[None, :]).astype(jnp.int32)
    running = jnp.cumsum(onehot, axis=0)
    position = jnp.sum(running * onehot, axis=1) - 1
    place = slot_list * MOST + position
    table = (jnp.arange(N_POOL * MOST, dtype=jnp.int32)[:, None] == place[None, :]).astype(jnp.float32)
    padded = jnp.dot(table, rows_x.astype(jnp.float32), precision=lax.Precision.HIGHEST).reshape(N_POOL, MOST, MODEL_WIDTH)
    shrink = jnp.einsum("smd,srd->smr", padded, down_pages).astype(jnp.bfloat16)
    adapter_delta = jnp.einsum("smr,sro->smo", shrink.astype(jnp.float32), up_pages).astype(jnp.bfloat16)
    return jnp.dot(table.T, adapter_delta.reshape(N_POOL * MOST, QUERY_FEATURES).astype(jnp.float32), precision=lax.Precision.HIGHEST)


def reference(tokens, query_weight, down_weight, up_weight, requests, row_slot_index):
    base = jnp.dot(tokens.reshape(STEPS * TOKENS, MODEL_WIDTH), query_weight, preferred_element_type=jnp.float32)
    grouped_rows = tokens.reshape(STEPS * N_POOL, ROWS, MODEL_WIDTH)
    wanted_pages = requests.reshape(STEPS * N_POOL, N_POOL)
    slot_list = row_slot_index.reshape(STEPS * N_POOL, ROWS)
    adapter_delta = lax.map(partial(grouped_delta, down_weight, up_weight), (grouped_rows, wanted_pages, slot_list))
    total = base + adapter_delta.reshape(STEPS * TOKENS, QUERY_FEATURES)
    return total.astype(jnp.bfloat16).reshape(STEPS, TOKENS, QUERY_FEATURES)
```

```python
import functools

import jax
import jax.numpy as jnp
from jax import lax
from jax.experimental import pallas as pl
from jax.experimental.pallas import tpu as pltpu
from jax.sharding import PartitionSpec as P

BF16 = jnp.bfloat16
F32 = jnp.float32
LANES = 128


def shrink_kernel(most, rank, ids_ref, x_ref, down_ref, out_ref, acc_ref):
    block, steps = x_ref.shape[0], x_ref.shape[1]
    first = pl.program_id(0) * block
    rows = x_ref[...].reshape(block * steps * most, x_ref.shape[-1])
    acc_ref[...] = lax.dot_general(
        rows, down_ref[...], (((1,), (0,)), ((), ())), preferred_element_type=F32
    )
    lane = lax.broadcasted_iota(jnp.int32, (most, LANES), 1)
    for i in range(block):
        parts = []
        for t in range(steps):
            adapter = ids_ref[first + i, t]
            column = pl.multiple_of((adapter // 2) * LANES, LANES)
            two = acc_ref[pl.ds((i * steps + t) * most, most), pl.ds(column, LANES)]
            swapped = pltpu.roll(two, rank, 1)
            parts.append(jnp.where(adapter % 2 == t, two, swapped))
        out_ref[i] = jnp.where(lane < rank, parts[0], parts[1]).astype(BF16)


def expand_kernel(most, rank, ids_ref, s_ref, up_ref, out_ref, wide_ref):
    block, steps = out_ref.shape[0], out_ref.shape[1]
    first = pl.program_id(0) * block
    wide_ref[...] = jnp.zeros_like(wide_ref)
    lane = lax.broadcasted_iota(jnp.int32, (most, LANES), 1)
    for i in range(block):
        both = s_ref[i].astype(F32)
        swapped = pltpu.roll(both, rank, 1)
        for t in range(steps):
            adapter = ids_ref[first + i, t]
            half = adapter % 2
            value = jnp.where(half == t, both, swapped)
            value = jnp.where((lane >= rank) == (half == 1), value, 0.0)
            column = pl.multiple_of((adapter // 2) * LANES, LANES)
            wide_ref[pl.ds((i * steps + t) * most, most), pl.ds(column, LANES)] = value.astype(BF16)
    out = jnp.dot(wide_ref[...], up_ref[...], preferred_element_type=F32)
    out_ref[...] = out.astype(BF16).reshape(out_ref.shape)


def shrink_rows(ids, x, down_t, block=8):
    groups, steps, most, width = x.shape
    held = down_t.shape[1]
    rank = LANES // 2
    return pl.pallas_call(
        functools.partial(shrink_kernel, most, rank),
        out_shape=jax.ShapeDtypeStruct((groups, most, steps * rank), BF16),
        grid_spec=pltpu.PrefetchScalarGridSpec(
            num_scalar_prefetch=1,
            grid=(groups // block,),
            in_specs=[
                pl.BlockSpec((block, steps, most, width), lambda i, ids: (i, 0, 0, 0)),
                pl.BlockSpec((width, held), lambda i, ids: (0, 0)),
            ],
            out_specs=pl.BlockSpec((block, most, steps * rank), lambda i, ids: (i, 0, 0)),
            scratch_shapes=[pltpu.VMEM((block * steps * most, held), F32)],
        ),
        compiler_params=pltpu.CompilerParams(vmem_limit_bytes=32 << 20),
        cost_estimate=pl.CostEstimate(
            flops=2 * groups * steps * most * width * held,
            bytes_accessed=2 * (x.size + down_t.size),
            transcendentals=0,
        ),
        name="shrink",
    )(ids, x, down_t)


def expand_rows(ids, s, up, steps, block=8):
    groups, most, both = s.shape
    held, features = up.shape
    rank = both // steps
    return pl.pallas_call(
        functools.partial(expand_kernel, most, rank),
        out_shape=jax.ShapeDtypeStruct((groups, steps, most, features), BF16),
        grid_spec=pltpu.PrefetchScalarGridSpec(
            num_scalar_prefetch=1,
            grid=(groups // block,),
            in_specs=[
                pl.BlockSpec((block, most, both), lambda i, ids: (i, 0, 0)),
                pl.BlockSpec((held, features), lambda i, ids: (0, 0)),
            ],
            out_specs=pl.BlockSpec((block, steps, most, features), lambda i, ids: (i, 0, 0, 0)),
            scratch_shapes=[pltpu.VMEM((block * steps * most, held), BF16)],
        ),
        compiler_params=pltpu.CompilerParams(vmem_limit_bytes=32 << 20),
        cost_estimate=pl.CostEstimate(
            flops=2 * groups * steps * most * held * features,
            bytes_accessed=2 * (s.size + up.size + groups * steps * most * features),
            transcendentals=0,
        ),
        name="expand",
    )(ids, s, up)


def sum_over_tp(partial_value):
    size = lax.axis_size("tp")
    groups, most, lanes = partial_value.shape
    flat = partial_value.reshape(groups * most, lanes)
    got = lax.all_to_all(flat, "tp", split_axis=0, concat_axis=0, tiled=True)
    share = got.reshape(size, groups * most // size, lanes).astype(F32).sum(0).astype(BF16)
    copies = jnp.broadcast_to(share[None], (size,) + share.shape).reshape(groups * most, lanes)
    full = lax.all_to_all(copies, "tp", split_axis=0, concat_axis=0, tiled=True)
    return full.reshape(groups, most, lanes)


def body(tokens, query_weight, down_weight, up_weight, requests, row_slot_index):
    count = lax.axis_size("pool")
    steps, rows, width = tokens.shape
    most = 4 * rows // count
    adapters, rank, _ = down_weight.shape
    features = up_weight.shape[-1]
    flat_tokens = tokens.reshape(steps * rows, width)

    slots = row_slot_index[:, 0, :]
    before = slots[:, None, :] < jnp.arange(count, dtype=jnp.int32)[None, :, None]
    start = jnp.minimum(jnp.sum(before.astype(jnp.int32), axis=2), rows - most)
    source = (
        jnp.arange(steps, dtype=jnp.int32)[None, :, None] * rows
        + start.T[:, :, None]
        + jnp.arange(most, dtype=jnp.int32)[None, None, :]
    ).reshape(count * steps * most)
    pick = (source[:, None] == jnp.arange(steps * rows, dtype=jnp.int32)[None, :]).astype(BF16)
    windows = jnp.dot(pick, flat_tokens, preferred_element_type=F32).astype(BF16)
    windows = windows.reshape(count, steps, most, width)
    x = lax.all_to_all(windows, "pool", split_axis=0, concat_axis=0, tiled=True)

    asked = lax.all_gather(requests[:, 0, :], "pool")
    ids = lax.dynamic_index_in_dim(asked, lax.axis_index("pool"), 2, False)

    base = jnp.dot(flat_tokens, query_weight, preferred_element_type=F32).astype(BF16)
    base_part = lax.psum_scatter(base, "tp", scatter_dimension=1, tiled=True)

    down_t = down_weight.reshape(adapters * rank, width).T
    shrink = sum_over_tp(shrink_rows(ids, x, down_t))
    delta = expand_rows(ids, shrink, up_weight.reshape(adapters * rank, features), steps)
    back = lax.all_to_all(delta, "pool", split_axis=0, concat_axis=0, tiled=True)

    mine = slots[:, :, None] == jnp.arange(count, dtype=jnp.int32)[None, None, :]
    own_start = jnp.sum(jnp.where(mine, start[:, None, :], 0), axis=2)
    place = (
        slots * (steps * most)
        + jnp.arange(steps, dtype=jnp.int32)[:, None] * most
        + jnp.arange(rows, dtype=jnp.int32)[None, :]
        - own_start
    ).reshape(steps * rows)
    spread = (place[:, None] == jnp.arange(count * steps * most, dtype=jnp.int32)[None, :]).astype(BF16)
    delta_rows = jnp.dot(
        spread, back.reshape(count * steps * most, features), preferred_element_type=F32
    )
    out = (base_part.astype(F32) + delta_rows).astype(BF16)
    return out.reshape(steps, rows, features)


def solution(mesh):
    placed = (
        P(None, "pool", "tp"),
        P("tp", None),
        P("pool", None, "tp"),
        P("pool", None, "tp"),
        P(None, "pool", None),
        P(None, "pool", None),
    )
    return jax.shard_map(
        body, mesh=mesh, in_specs=placed, out_specs=P(None, "pool", "tp"), check_vma=False
    )
```

```python
import functools

import jax
import jax.numpy as jnp
from jax import lax
from jax.experimental import pallas as pl
from jax.experimental.pallas import tpu as pltpu
from jax.sharding import PartitionSpec as P

BF16 = jnp.bfloat16
F32 = jnp.float32
LANES = 128
TILE = 16
VMEM = 40 << 20


def pack_kernel(asked_ref, slots_ref, tokens_ref, out_ref):
    steps, rows, width = tokens_ref.shape
    block, tiles = out_ref.shape[0], out_ref.shape[1] - 1
    across = width // LANES
    most = tiles // (steps * across) * TILE
    first = pl.program_id(0) * block
    shape = (block, most, rows)
    slot = lax.broadcasted_iota(jnp.int32, shape, 0) + first
    ahead = lax.broadcasted_iota(jnp.int32, shape, 1)
    position = lax.broadcasted_iota(jnp.int32, shape, 2)
    for t in range(steps):
        held = jnp.broadcast_to(slots_ref[t].reshape(1, 1, rows), shape)
        before = jnp.where(held < slot, 1.0, 0.0)
        start = jnp.minimum(jnp.sum(before, axis=2, keepdims=True).astype(jnp.int32), rows - most)
        pick = jnp.where(position == start + ahead, 1.0, 0.0).astype(BF16)
        value = jnp.dot(pick.reshape(block * most, rows), tokens_ref[t], preferred_element_type=F32)
        value = value.astype(BF16).reshape(block, most // TILE, TILE, width)
        for down in range(most // TILE):
            for c in range(across):
                tile = (t * (most // TILE) + down) * across + c
                out_ref[:, tile] = value[:, down, :, c * LANES : (c + 1) * LANES]
    line = lax.broadcasted_iota(jnp.int32, (TILE, LANES), 0)
    for s in range(block):
        names = jnp.where(line < TILE // 2, asked_ref[0, first + s], asked_ref[1, first + s])
        out_ref[s, tiles] = names.astype(F32).astype(BF16)


def pack(asked, slots, tokens, most, block=8):
    steps, rows, width = tokens.shape
    count = asked.shape[1]
    tiles = steps * (most // TILE) * (width // LANES)
    return pl.pallas_call(
        pack_kernel,
        out_shape=jax.ShapeDtypeStruct((count, tiles + 1, TILE, LANES), BF16),
        grid_spec=pltpu.PrefetchScalarGridSpec(
            num_scalar_prefetch=1,
            grid=(count // block,),
            in_specs=[
                pl.BlockSpec((steps, 1, rows), lambda i, asked: (0, 0, 0)),
                pl.BlockSpec((steps, rows, width), lambda i, asked: (0, 0, 0)),
            ],
            out_specs=pl.BlockSpec((block, tiles + 1, TILE, LANES), lambda i, asked: (i, 0, 0, 0)),
        ),
        compiler_params=pltpu.CompilerParams(vmem_limit_bytes=VMEM),
        cost_estimate=pl.CostEstimate(
            flops=2 * count * steps * most * rows * width,
            bytes_accessed=2 * (tokens.size + count * (tiles + 1) * TILE * LANES),
            transcendentals=0,
        ),
        name="pack",
    )(asked, slots, tokens)


def shrink_kernel(rank, names_ref, x_ref, down_ref, out_ref, rows_ref, acc_ref):
    block, steps, most, held = acc_ref.shape
    width = rows_ref.shape[-1]
    across = width // LANES
    for d in range(rows_ref.shape[1]):
        for c in range(across):
            rows_ref[:, d, :, c * LANES : (c + 1) * LANES] = x_ref[:, d * across + c]
    acc = jnp.dot(rows_ref[...].reshape(block * steps * most, width), down_ref[...], preferred_element_type=F32)
    acc_ref[...] = acc.reshape(acc_ref.shape)
    names = names_ref[:, 0].astype(F32)
    lane = lax.broadcasted_iota(jnp.int32, (block * most, LANES), 1)
    parts = []
    for t in range(steps):
        wanted = names[:, t * (TILE // steps) : t * (TILE // steps) + 1, :]
        wanted = jnp.broadcast_to(wanted, (block, most, LANES))
        value = jnp.zeros((block, most, LANES), F32)
        odd = jnp.zeros((block, most, LANES), F32)
        for c in range(held // LANES):
            here = acc_ref[:, t, :, c * LANES : (c + 1) * LANES]
            value = jnp.where((wanted == 2.0 * c) | (wanted == 2.0 * c + 1.0), here, value)
            odd = jnp.where(wanted == 2.0 * c + 1.0, 1.0, odd)
        value = value.reshape(block * most, LANES)
        odd = odd.reshape(block * most, LANES)
        parts.append(jnp.where(odd == 1.0 * t, value, pltpu.roll(value, rank, 1)))
    out = jnp.where(lane < rank, parts[0], parts[1])
    out_ref[...] = out.astype(BF16).reshape(out_ref.shape)


def shrink_rows(x, down_t, steps, most, rank, block=8):
    groups, tiles = x.shape[0], x.shape[1] - 1
    width, held = down_t.shape
    return pl.pallas_call(
        functools.partial(shrink_kernel, rank),
        out_shape=jax.ShapeDtypeStruct((groups, most, LANES), BF16),
        grid=(groups // block,),
        in_specs=[
            pl.BlockSpec((block, 1, TILE, LANES), lambda i: (i, tiles, 0, 0)),
            pl.BlockSpec((block, tiles, TILE, LANES), lambda i: (i, 0, 0, 0)),
            pl.BlockSpec((width, held), lambda i: (0, 0)),
        ],
        out_specs=pl.BlockSpec((block, most, LANES), lambda i: (i, 0, 0)),
        scratch_shapes=[
            pltpu.VMEM((block, steps * most // TILE, TILE, width), BF16),
            pltpu.VMEM((block, steps, most, held), F32),
        ],
        compiler_params=pltpu.CompilerParams(vmem_limit_bytes=VMEM),
        cost_estimate=pl.CostEstimate(
            flops=2 * groups * steps * most * width * held,
            bytes_accessed=2 * (x.size + down_t.size),
            transcendentals=0,
        ),
        name="shrink",
    )(x, x, down_t)


def expand_kernel(rank, names_ref, s_ref, up_ref, out_ref, wide_ref):
    block, steps, most, held = wide_ref.shape
    names = names_ref[:, 0].astype(F32)
    both = s_ref[...].astype(F32).reshape(block * most, LANES)
    swapped = pltpu.roll(both, rank, 1).reshape(block, most, LANES)
    both = both.reshape(block, most, LANES)
    high = jnp.where(lax.broadcasted_iota(jnp.int32, (block, most, LANES), 2) < rank, 0.0, 1.0)
    for t in range(steps):
        wanted = names[:, t * (TILE // steps) : t * (TILE // steps) + 1, :]
        wanted = jnp.broadcast_to(wanted, (block, most, LANES))
        for c in range(held // LANES):
            chosen = jnp.where(high == 1.0 * t, both, swapped)
            value = jnp.where(wanted == 2.0 * c + high, chosen, 0.0)
            wide_ref[:, t, :, c * LANES : (c + 1) * LANES] = value.astype(BF16)
    wide = wide_ref[...].reshape(block * steps * most, held)
    out = jnp.dot(wide, up_ref[...], preferred_element_type=F32)
    out_ref[...] = out.astype(BF16).reshape(out_ref.shape)


def expand_rows(x, s, up, steps, rank, block=8):
    groups, most, _ = s.shape
    tiles = x.shape[1] - 1
    held, features = up.shape
    return pl.pallas_call(
        functools.partial(expand_kernel, rank),
        out_shape=jax.ShapeDtypeStruct((groups, steps, most, features), BF16),
        grid=(groups // block,),
        in_specs=[
            pl.BlockSpec((block, 1, TILE, LANES), lambda i: (i, tiles, 0, 0)),
            pl.BlockSpec((block, most, LANES), lambda i: (i, 0, 0)),
            pl.BlockSpec((held, features), lambda i: (0, 0)),
        ],
        out_specs=pl.BlockSpec((block, steps, most, features), lambda i: (i, 0, 0, 0)),
        scratch_shapes=[pltpu.VMEM((block, steps, most, held), BF16)],
        compiler_params=pltpu.CompilerParams(vmem_limit_bytes=VMEM),
        cost_estimate=pl.CostEstimate(
            flops=2 * groups * steps * most * held * features,
            bytes_accessed=2 * (s.size + up.size + groups * steps * most * features),
            transcendentals=0,
        ),
        name="expand",
    )(x, s, up)


def shares_kernel(order_ref, tokens_ref, weight_ref, out_ref):
    out_ref[0] = jnp.dot(tokens_ref[...], weight_ref[...], preferred_element_type=F32)


def base_shares(flat_tokens, query_weight):
    size = lax.axis_size("tp")
    rows, width = flat_tokens.shape
    columns = query_weight.shape[1] // size
    order = lax.rem(lax.axis_index("tp") + jnp.arange(size, dtype=jnp.int32), size)
    return pl.pallas_call(
        shares_kernel,
        out_shape=jax.ShapeDtypeStruct((size, rows, columns), F32),
        grid_spec=pltpu.PrefetchScalarGridSpec(
            num_scalar_prefetch=1,
            grid=(size,),
            in_specs=[
                pl.BlockSpec((rows, width), lambda k, order: (0, 0)),
                pl.BlockSpec((width, columns), lambda k, order: (0, order[k])),
            ],
            out_specs=pl.BlockSpec((1, rows, columns), lambda k, order: (k, 0, 0)),
        ),
        compiler_params=pltpu.CompilerParams(vmem_limit_bytes=VMEM),
        cost_estimate=pl.CostEstimate(
            flops=2 * rows * width * columns * size,
            bytes_accessed=2 * query_weight.size + 4 * rows * columns * size,
            transcendentals=0,
        ),
        name="shares",
    )(order, flat_tokens, query_weight)


def sum_over_tp(partial_value):
    size = lax.axis_size("tp")
    groups, most, lanes = partial_value.shape
    flat = partial_value.reshape(groups * most, lanes)
    got = lax.all_to_all(flat, "tp", split_axis=0, concat_axis=0, tiled=True)
    share = got.reshape(size, groups * most // size, lanes).astype(F32).sum(0).astype(BF16)
    copies = jnp.broadcast_to(share[None], (size,) + share.shape).reshape(groups * most, lanes)
    full = lax.all_to_all(copies, "tp", split_axis=0, concat_axis=0, tiled=True)
    return full.reshape(groups, most, lanes)


def body(tokens, query_weight, down_weight, up_weight, requests, row_slot_index):
    count = lax.axis_size("pool")
    size = lax.axis_size("tp")
    steps, rows, width = tokens.shape
    most = 4 * rows // count
    adapters, rank, _ = down_weight.shape
    features = up_weight.shape[-1]
    middle = steps * rows // 2
    right = [(i, (i + 1) % size) for i in range(size)]
    left = [(i, (i - 1) % size) for i in range(size)]

    sent = pack(requests[:, 0, :], row_slot_index, tokens, most)
    sent, late_tokens, late_slots = lax.optimization_barrier((sent, tokens, row_slot_index))
    x = lax.all_to_all(sent, "pool", split_axis=0, concat_axis=0, tiled=True)

    shares = base_shares(late_tokens.reshape(steps * rows, width), query_weight)
    far = size // 2
    top = lax.ppermute(shares[far, :middle].astype(BF16), "tp", right).astype(F32)
    low = lax.ppermute(shares[far, middle:].astype(BF16), "tp", left).astype(F32)
    going_right = jnp.concatenate([shares[far - 1, :middle] + top, shares[far - 1, middle:]], 0)
    going_left = jnp.concatenate([shares[far + 1, :middle], shares[far + 1, middle:] + low], 0)
    for ahead in range(far - 2, 0, -1):
        going_right = lax.ppermute(going_right.astype(BF16), "tp", right).astype(F32) + shares[ahead]
        going_left = lax.ppermute(going_left.astype(BF16), "tp", left).astype(F32) + shares[size - ahead]
    going_right, going_left = going_right.astype(BF16), going_left.astype(BF16)

    down_t = down_weight.reshape(adapters * rank, width).T
    shrink = sum_over_tp(shrink_rows(x, down_t, steps, most, rank))
    delta = expand_rows(x, shrink, up_weight.reshape(adapters * rank, features), steps, rank)
    delta, going_right, going_left = lax.optimization_barrier((delta, going_right, going_left))
    back = lax.all_to_all(delta, "pool", split_axis=0, concat_axis=0, tiled=True)
    from_left = lax.ppermute(going_right, "tp", right).astype(F32)
    from_right = lax.ppermute(going_left, "tp", left).astype(F32)
    base = shares[0] + from_left + from_right

    slots = late_slots[:, 0, :]
    before = slots[:, None, :] < jnp.arange(count, dtype=jnp.int32)[None, :, None]
    start = jnp.minimum(jnp.sum(before.astype(jnp.int32), axis=2), rows - most)
    mine = slots[:, :, None] == jnp.arange(count, dtype=jnp.int32)[None, None, :]
    own_start = jnp.sum(jnp.where(mine, start[:, None, :], 0), axis=2)
    place = (
        slots * (steps * most)
        + jnp.arange(steps, dtype=jnp.int32)[:, None] * most
        + jnp.arange(rows, dtype=jnp.int32)[None, :]
        - own_start
    ).reshape(steps * rows)
    spread = (place[:, None] == jnp.arange(count * steps * most, dtype=jnp.int32)[None, :]).astype(BF16)
    delta_rows = jnp.dot(
        spread, back.reshape(count * steps * most, features), preferred_element_type=F32
    )
    return (base + delta_rows).astype(BF16).reshape(steps, rows, features)


def solution(mesh):
    placed = (
        P(None, "pool", "tp"),
        P("tp", None),
        P("pool", None, "tp"),
        P("pool", None, "tp"),
        P(None, "pool", None),
        P(None, "pool", None),
    )
    return jax.shard_map(
        body, mesh=mesh, in_specs=placed, out_specs=P(None, "pool", "tp"), check_vma=False
    )
```

```python
import functools

import jax
import jax.numpy as jnp
from jax import lax
from jax.experimental import pallas as pl
from jax.experimental.pallas import tpu as pltpu
from jax.sharding import PartitionSpec as P

BF16 = jnp.bfloat16
F32 = jnp.float32
LANES = 128
TILE = 16
VMEM = 24 << 20
FULL = 62 << 20


def pack_kernel(asked_ref, slots_ref, tokens_ref, out_ref):
    steps, rows, width = tokens_ref.shape
    block, tiles = out_ref.shape[0], out_ref.shape[1] - 1
    across = width // LANES
    most = tiles // (steps * across) * TILE
    first = pl.program_id(0) * block
    shape = (block, most, rows)
    slot = lax.broadcasted_iota(jnp.int32, shape, 0) + first
    ahead = lax.broadcasted_iota(jnp.int32, shape, 1)
    position = lax.broadcasted_iota(jnp.int32, shape, 2)
    for t in range(steps):
        held = jnp.broadcast_to(slots_ref[t].reshape(1, 1, rows), shape)
        before = jnp.where(held < slot, 1.0, 0.0)
        start = jnp.minimum(jnp.sum(before, axis=2, keepdims=True).astype(jnp.int32), rows - most)
        pick = jnp.where(position == start + ahead, 1.0, 0.0).astype(BF16)
        value = jnp.dot(pick.reshape(block * most, rows), tokens_ref[t], preferred_element_type=F32)
        value = value.astype(BF16).reshape(block, most // TILE, TILE, width)
        for down in range(most // TILE):
            for c in range(across):
                tile = (t * (most // TILE) + down) * across + c
                out_ref[:, tile] = value[:, down, :, c * LANES : (c + 1) * LANES]
    line = lax.broadcasted_iota(jnp.int32, (TILE, LANES), 0)
    for s in range(block):
        names = jnp.where(line < TILE // 2, asked_ref[0, first + s], asked_ref[1, first + s])
        out_ref[s, tiles] = names.astype(F32).astype(BF16)


def pack(asked, slots, tokens, most, block=16):
    steps, rows, width = tokens.shape
    count = asked.shape[1]
    tiles = steps * (most // TILE) * (width // LANES)
    return pl.pallas_call(
        pack_kernel,
        out_shape=jax.ShapeDtypeStruct((count, tiles + 1, TILE, LANES), BF16),
        grid_spec=pltpu.PrefetchScalarGridSpec(
            num_scalar_prefetch=1,
            grid=(count // block,),
            in_specs=[
                pl.BlockSpec((steps, 1, rows), lambda i, asked: (0, 0, 0)),
                pl.BlockSpec((steps, rows, width), lambda i, asked: (0, 0, 0)),
            ],
            out_specs=pl.BlockSpec((block, tiles + 1, TILE, LANES), lambda i, asked: (i, 0, 0, 0)),
        ),
        compiler_params=pltpu.CompilerParams(vmem_limit_bytes=FULL),
        cost_estimate=pl.CostEstimate(
            flops=2 * count * steps * most * rows * width,
            bytes_accessed=2 * (tokens.size + count * (tiles + 1) * TILE * LANES),
            transcendentals=0,
        ),
        name="pack",
    )(asked, slots, tokens)


def shrink_kernel(rank, names_ref, x_ref, down_ref, out_ref, rows_ref, acc_ref):
    block, steps, most, held = acc_ref.shape
    width = rows_ref.shape[-1]
    across = width // LANES
    for d in range(rows_ref.shape[1]):
        for c in range(across):
            rows_ref[:, d, :, c * LANES : (c + 1) * LANES] = x_ref[:, d * across + c]
    acc = jnp.dot(rows_ref[...].reshape(block * steps * most, width), down_ref[...], preferred_element_type=F32)
    acc_ref[...] = acc.reshape(acc_ref.shape)
    names = names_ref[:, 0].astype(F32)
    lane = lax.broadcasted_iota(jnp.int32, (block * most, LANES), 1)
    parts = []
    for t in range(steps):
        wanted = names[:, t * (TILE // steps) : t * (TILE // steps) + 1, :]
        wanted = jnp.broadcast_to(wanted, (block, most, LANES))
        value = jnp.zeros((block, most, LANES), F32)
        odd = jnp.zeros((block, most, LANES), F32)
        for c in range(held // LANES):
            here = acc_ref[:, t, :, c * LANES : (c + 1) * LANES]
            value = jnp.where((wanted == 2.0 * c) | (wanted == 2.0 * c + 1.0), here, value)
            odd = jnp.where(wanted == 2.0 * c + 1.0, 1.0, odd)
        value = value.reshape(block * most, LANES)
        odd = odd.reshape(block * most, LANES)
        parts.append(jnp.where(odd == 1.0 * t, value, pltpu.roll(value, rank, 1)))
    out = jnp.where(lane < rank, parts[0], parts[1])
    out_ref[...] = out.astype(BF16).reshape(out_ref.shape)


def shrink_rows(x, down_t, steps, most, rank, block=16):
    groups, tiles = x.shape[0], x.shape[1] - 1
    width, held = down_t.shape
    return pl.pallas_call(
        functools.partial(shrink_kernel, rank),
        out_shape=jax.ShapeDtypeStruct((groups, most, LANES), BF16),
        grid=(groups // block,),
        in_specs=[
            pl.BlockSpec((block, 1, TILE, LANES), lambda i: (i, tiles, 0, 0)),
            pl.BlockSpec((block, tiles, TILE, LANES), lambda i: (i, 0, 0, 0)),
            pl.BlockSpec((width, held), lambda i: (0, 0)),
        ],
        out_specs=pl.BlockSpec((block, most, LANES), lambda i: (i, 0, 0)),
        scratch_shapes=[
            pltpu.VMEM((block, steps * most // TILE, TILE, width), BF16),
            pltpu.VMEM((block, steps, most, held), F32),
        ],
        compiler_params=pltpu.CompilerParams(vmem_limit_bytes=VMEM),
        cost_estimate=pl.CostEstimate(
            flops=2 * groups * steps * most * width * held,
            bytes_accessed=2 * (x.size + down_t.size),
            transcendentals=0,
        ),
        name="shrink",
    )(x, x, down_t)


def expand_kernel(rank, names_ref, s_ref, up_ref, out_ref, wide_ref):
    block, steps, most, held = wide_ref.shape
    names = names_ref[:, 0].astype(F32)
    both = s_ref[...].astype(F32).reshape(block * most, LANES)
    swapped = pltpu.roll(both, rank, 1).reshape(block, most, LANES)
    both = both.reshape(block, most, LANES)
    high = jnp.where(lax.broadcasted_iota(jnp.int32, (block, most, LANES), 2) < rank, 0.0, 1.0)
    for t in range(steps):
        wanted = names[:, t * (TILE // steps) : t * (TILE // steps) + 1, :]
        wanted = jnp.broadcast_to(wanted, (block, most, LANES))
        for c in range(held // LANES):
            chosen = jnp.where(high == 1.0 * t, both, swapped)
            value = jnp.where(wanted == 2.0 * c + high, chosen, 0.0)
            wide_ref[:, t, :, c * LANES : (c + 1) * LANES] = value.astype(BF16)
    wide = wide_ref[...].reshape(block * steps * most, held)
    out = jnp.dot(wide, up_ref[...], preferred_element_type=F32)
    out_ref[...] = out.astype(BF16).reshape(out_ref.shape)


def expand_rows(x, s, up, steps, rank, block=8):
    groups, most, _ = s.shape
    tiles = x.shape[1] - 1
    held, features = up.shape
    return pl.pallas_call(
        functools.partial(expand_kernel, rank),
        out_shape=jax.ShapeDtypeStruct((groups, steps, most, features), BF16),
        grid=(groups // block,),
        in_specs=[
            pl.BlockSpec((block, 1, TILE, LANES), lambda i: (i, tiles, 0, 0)),
            pl.BlockSpec((block, most, LANES), lambda i: (i, 0, 0)),
            pl.BlockSpec((held, features), lambda i: (0, 0)),
        ],
        out_specs=pl.BlockSpec((block, steps, most, features), lambda i: (i, 0, 0, 0)),
        scratch_shapes=[pltpu.VMEM((block, steps, most, held), BF16)],
        compiler_params=pltpu.CompilerParams(vmem_limit_bytes=FULL),
        cost_estimate=pl.CostEstimate(
            flops=2 * groups * steps * most * held * features,
            bytes_accessed=2 * (s.size + up.size + groups * steps * most * features),
            transcendentals=0,
        ),
        name="expand",
    )(x, s, up)


def shares_kernel(order_ref, tokens_ref, weight_ref, out_ref):
    out_ref[0] = jnp.dot(tokens_ref[...], weight_ref[...], preferred_element_type=F32)


def base_shares(flat_tokens, query_weight, distances):
    size = lax.axis_size("tp")
    rows, width = flat_tokens.shape
    columns = query_weight.shape[1] // size
    order = lax.rem(lax.axis_index("tp") + jnp.array(distances, jnp.int32), size)
    amount = len(distances)
    return pl.pallas_call(
        shares_kernel,
        out_shape=jax.ShapeDtypeStruct((amount, rows, columns), F32),
        grid_spec=pltpu.PrefetchScalarGridSpec(
            num_scalar_prefetch=1,
            grid=(amount,),
            in_specs=[
                pl.BlockSpec((rows, width), lambda k, order: (0, 0)),
                pl.BlockSpec((width, columns), lambda k, order: (0, order[k])),
            ],
            out_specs=pl.BlockSpec((1, rows, columns), lambda k, order: (k, 0, 0)),
        ),
        compiler_params=pltpu.CompilerParams(vmem_limit_bytes=VMEM),
        cost_estimate=pl.CostEstimate(
            flops=2 * rows * width * columns * amount,
            bytes_accessed=2 * width * columns * amount + 4 * rows * columns * amount,
            transcendentals=0,
        ),
        name="shares",
    )(order, flat_tokens, query_weight)


def first_sums_kernel(shares_ref, top_ref, low_ref, right_ref, left_ref):
    middle = top_ref.shape[0]
    right_ref[:middle] = (shares_ref[0, :middle] + top_ref[...].astype(F32)).astype(BF16)
    right_ref[middle:] = shares_ref[0, middle:].astype(BF16)
    left_ref[:middle] = shares_ref[1, :middle].astype(BF16)
    left_ref[middle:] = (shares_ref[1, middle:] + low_ref[...].astype(F32)).astype(BF16)


def first_sums(shares, top, low):
    _, rows, columns = shares.shape
    out = jax.ShapeDtypeStruct((rows, columns), BF16)
    return pl.pallas_call(
        first_sums_kernel,
        out_shape=(out, out),
        compiler_params=pltpu.CompilerParams(vmem_limit_bytes=VMEM),
        cost_estimate=pl.CostEstimate(
            flops=2 * rows * columns, bytes_accessed=14 * rows * columns, transcendentals=0
        ),
        name="first_sums",
    )(shares, top, low)


def join_kernel(spread_ref, back_ref, base_ref, out_ref):
    groups, _, most, features = back_ref.shape
    back = back_ref[...].reshape(groups * most, features)
    delta = jnp.dot(spread_ref[0], back, preferred_element_type=F32)
    out_ref[0] = (base_ref[0] + delta).astype(BF16)


def join(spread, back, base):
    steps, rows, places = spread.shape
    groups, _, most, features = back.shape
    return pl.pallas_call(
        join_kernel,
        out_shape=jax.ShapeDtypeStruct((steps, rows, features), BF16),
        grid=(steps,),
        in_specs=[
            pl.BlockSpec((1, rows, places), lambda t: (t, 0, 0)),
            pl.BlockSpec((groups, 1, most, features), lambda t: (0, t, 0, 0)),
            pl.BlockSpec((1, rows, features), lambda t: (t, 0, 0)),
        ],
        out_specs=pl.BlockSpec((1, rows, features), lambda t: (t, 0, 0)),
        compiler_params=pltpu.CompilerParams(vmem_limit_bytes=FULL),
        cost_estimate=pl.CostEstimate(
            flops=2 * steps * rows * places * features,
            bytes_accessed=2 * (spread.size + back.size) + 6 * base.size,
            transcendentals=0,
        ),
        name="join",
    )(spread, back, base)


def sum_over_tp(partial_value):
    size = lax.axis_size("tp")
    groups, most, lanes = partial_value.shape
    flat = partial_value.reshape(groups * most, lanes)
    got = lax.all_to_all(flat, "tp", split_axis=0, concat_axis=0, tiled=True)
    share = got.reshape(size, groups * most // size, lanes).astype(F32).sum(0).astype(BF16)
    copies = jnp.broadcast_to(share[None], (size,) + share.shape).reshape(groups * most, lanes)
    full = lax.all_to_all(copies, "tp", split_axis=0, concat_axis=0, tiled=True)
    return full.reshape(groups, most, lanes)


def body(tokens, query_weight, down_weight, up_weight, requests, row_slot_index):
    count = lax.axis_size("pool")
    size = lax.axis_size("tp")
    steps, rows, width = tokens.shape
    most = 4 * rows // count
    adapters, rank, _ = down_weight.shape
    features = up_weight.shape[-1]
    middle = steps * rows // 2
    right = [(i, (i + 1) % size) for i in range(size)]
    left = [(i, (i - 1) % size) for i in range(size)]

    sent = pack(requests[:, 0, :], row_slot_index, tokens, most)
    sent, late_tokens, late_slots = lax.optimization_barrier((sent, tokens, row_slot_index))
    x = lax.all_to_all(sent, "pool", split_axis=0, concat_axis=0, tiled=True)

    late_tokens = late_tokens.reshape(steps * rows, width)
    far = size // 2
    farthest = base_shares(late_tokens, query_weight, [far])[0].astype(BF16)
    top = lax.ppermute(farthest[:middle], "tp", right)
    low = lax.ppermute(farthest[middle:], "tp", left)
    late_tokens, _ = lax.optimization_barrier((late_tokens, farthest))
    near = [d for ahead in range(far - 2, 0, -1) for d in (ahead, size - ahead)] + [0]
    first = base_shares(late_tokens, query_weight, [far - 1, far + 1])
    late_tokens, first = lax.optimization_barrier((late_tokens, first))
    going_right, going_left = first_sums(first, top, low)
    shares = base_shares(late_tokens, query_weight, near)
    for hop in range(far - 2):
        going_right = lax.ppermute(going_right, "tp", right).astype(F32) + shares[2 * hop]
        going_left = lax.ppermute(going_left, "tp", left).astype(F32) + shares[2 * hop + 1]
        going_right, going_left = going_right.astype(BF16), going_left.astype(BF16)
    x, going_right, going_left = lax.optimization_barrier((x, going_right, going_left))

    down_t = down_weight.reshape(adapters * rank, width).T
    shrink = sum_over_tp(shrink_rows(x, down_t, steps, most, rank))
    delta = expand_rows(x, shrink, up_weight.reshape(adapters * rank, features), steps, rank)
    delta, going_right, going_left = lax.optimization_barrier((delta, going_right, going_left))
    back = lax.all_to_all(delta, "pool", split_axis=0, concat_axis=0, tiled=True)
    from_left = lax.ppermute(going_right, "tp", right).astype(F32)
    from_right = lax.ppermute(going_left, "tp", left).astype(F32)
    base = (shares[-1] + from_left + from_right).reshape(steps, rows, features)

    slots = late_slots[:, 0, :]
    before = slots[:, None, :] < jnp.arange(count, dtype=jnp.int32)[None, :, None]
    start = jnp.minimum(jnp.sum(before.astype(jnp.int32), axis=2), rows - most)
    mine = slots[:, :, None] == jnp.arange(count, dtype=jnp.int32)[None, None, :]
    own_start = jnp.sum(jnp.where(mine, start[:, None, :], 0), axis=2)
    place = slots * most + jnp.arange(rows, dtype=jnp.int32)[None, :] - own_start
    spread = (place[:, :, None] == jnp.arange(count * most, dtype=jnp.int32)[None, None, :]).astype(BF16)
    return join(spread, back, base)


def solution(mesh):
    placed = (
        P(None, "pool", "tp"),
        P("tp", None),
        P("pool", None, "tp"),
        P("pool", None, "tp"),
        P(None, "pool", None),
        P(None, "pool", None),
    )
    return jax.shard_map(
        body, mesh=mesh, in_specs=placed, out_specs=P(None, "pool", "tp"), check_vma=False
    )
```

```python
import functools

import jax
import jax.numpy as jnp
from jax import lax
from jax.experimental import pallas as pl
from jax.experimental.pallas import tpu as pltpu
from jax.sharding import PartitionSpec as P

BF16 = jnp.bfloat16
F32 = jnp.float32
LANES = 128
TILE = 16
VMEM = 18 << 20
FULL = 62 << 20


def pack_kernel(step, asked_ref, slots_ref, tokens_ref, out_ref):
    rows, width = tokens_ref.shape[1:]
    block = out_ref.shape[0]
    across = width // LANES
    most = out_ref.shape[1] // across * TILE
    first = pl.program_id(0) * block
    shape = (block, most, rows)
    slot = lax.broadcasted_iota(jnp.int32, shape, 0) + first
    ahead = lax.broadcasted_iota(jnp.int32, shape, 1)
    position = lax.broadcasted_iota(jnp.int32, shape, 2)
    held = jnp.broadcast_to(slots_ref[0].reshape(1, 1, rows), shape)
    before = jnp.where(held < slot, 1.0, 0.0)
    start = jnp.minimum(jnp.sum(before, axis=2, keepdims=True).astype(jnp.int32), rows - most)
    pick = jnp.where(position == start + ahead, 1.0, 0.0).astype(BF16)
    value = jnp.dot(pick.reshape(block * most, rows), tokens_ref[0], preferred_element_type=F32)
    value = value.astype(BF16).reshape(block, most // TILE, TILE, width)
    for down in range(most // TILE):
        for c in range(across):
            out_ref[:, down * across + c] = value[:, down, :, c * LANES : (c + 1) * LANES]
    if step == 0:
        line = lax.broadcasted_iota(jnp.int32, (TILE, LANES), 0)
        for s in range(block):
            names = jnp.where(line < TILE // 2, asked_ref[0, first + s], asked_ref[1, first + s])
            out_ref[s, most // TILE * across] = names.astype(F32).astype(BF16)


def pack(step, asked, slots, tokens, most, block=16):
    _, rows, width = tokens.shape
    count = asked.shape[1]
    tiles = (most // TILE) * (width // LANES) + (1 if step == 0 else 0)
    return pl.pallas_call(
        functools.partial(pack_kernel, step),
        out_shape=jax.ShapeDtypeStruct((count, tiles, TILE, LANES), BF16),
        grid_spec=pltpu.PrefetchScalarGridSpec(
            num_scalar_prefetch=1,
            grid=(count // block,),
            in_specs=[
                pl.BlockSpec((1, 1, rows), lambda i, asked: (step, 0, 0)),
                pl.BlockSpec((1, rows, width), lambda i, asked: (step, 0, 0)),
            ],
            out_specs=pl.BlockSpec((block, tiles, TILE, LANES), lambda i, asked: (i, 0, 0, 0)),
        ),
        compiler_params=pltpu.CompilerParams(vmem_limit_bytes=FULL if step == 0 else VMEM),
        cost_estimate=pl.CostEstimate(
            flops=2 * count * most * rows * width,
            bytes_accessed=2 * (rows * width + count * tiles * TILE * LANES),
            transcendentals=0,
        ),
        name="pack",
    )(asked, slots, tokens)


def named(names_ref, step, half, block, most):
    line = step * (TILE // 2)
    return jnp.broadcast_to(
        names_ref[half, :, 0].astype(F32)[:, line : line + 1, :], (block, most, LANES)
    )


def shrink_kernel(step, rank, names_ref, x_ref, down_ref, out_ref, rows_ref, acc_ref):
    halves, block, most, held = acc_ref.shape
    width = rows_ref.shape[-1]
    across = width // LANES
    for d in range(rows_ref.shape[2]):
        for c in range(across):
            rows_ref[:, :, d, :, c * LANES : (c + 1) * LANES] = x_ref[:, :, d * across + c]
    acc = lax.dot_general(
        rows_ref[...].reshape(halves * block * most, width),
        down_ref[...],
        (((1,), (1,)), ((), ())),
        preferred_element_type=F32,
    )
    acc_ref[...] = acc.reshape(acc_ref.shape)
    lane = lax.broadcasted_iota(jnp.int32, (block * most, LANES), 1)
    parts = []
    for h in range(halves):
        wanted = named(names_ref, step, h, block, most)
        value = jnp.zeros((block, most, LANES), F32)
        odd = jnp.zeros((block, most, LANES), F32)
        for c in range(held // LANES):
            here = acc_ref[h, :, :, c * LANES : (c + 1) * LANES]
            value = jnp.where((wanted == 2.0 * c) | (wanted == 2.0 * c + 1.0), here, value)
            odd = jnp.where(wanted == 2.0 * c + 1.0, 1.0, odd)
        value = value.reshape(block * most, LANES)
        odd = odd.reshape(block * most, LANES)
        parts.append(jnp.where(odd == 1.0 * h, value, pltpu.roll(value, rank, 1)))
    out = jnp.where(lane < rank, parts[0], parts[1])
    out_ref[...] = out.astype(BF16).reshape(out_ref.shape)


def shrink_rows(step, names, x, down, most, rank, block=8):
    half = x.shape[0] // 2
    held, width = down.shape
    tiles = (most // TILE) * (width // LANES)
    names = names.reshape((2, half) + names.shape[1:])
    x = x.reshape((2, half) + x.shape[1:])
    return pl.pallas_call(
        functools.partial(shrink_kernel, step, rank),
        out_shape=jax.ShapeDtypeStruct((half, most, LANES), BF16),
        grid=(half // block,),
        in_specs=[
            pl.BlockSpec((2, block, 1, TILE, LANES), lambda i: (0, i, tiles, 0, 0)),
            pl.BlockSpec((2, block, tiles, TILE, LANES), lambda i: (0, i, 0, 0, 0)),
            pl.BlockSpec((held, width), lambda i: (0, 0)),
        ],
        out_specs=pl.BlockSpec((block, most, LANES), lambda i: (i, 0, 0)),
        scratch_shapes=[
            pltpu.VMEM((2, block, most // TILE, TILE, width), BF16),
            pltpu.VMEM((2, block, most, held), F32),
        ],
        compiler_params=pltpu.CompilerParams(vmem_limit_bytes=VMEM),
        cost_estimate=pl.CostEstimate(
            flops=4 * half * most * width * held,
            bytes_accessed=2 * (x.size + down.size),
            transcendentals=0,
        ),
        name="shrink",
    )(names, x, down)


def expand_kernel(step, rank, names_ref, a_ref, b_ref, c_ref, d_ref, e_ref, up_ref, out_ref, wide_ref):
    halves, block, most, held = wide_ref.shape
    both = a_ref[...].astype(F32)
    for ref in (b_ref, c_ref, d_ref, e_ref):
        both = both + ref[...].astype(F32)
    swapped = pltpu.roll(both.reshape(block * most, LANES), rank, 1).reshape(block, most, LANES)
    high = jnp.where(lax.broadcasted_iota(jnp.int32, (block, most, LANES), 2) < rank, 0.0, 1.0)
    for h in range(halves):
        wanted = named(names_ref, step, h, block, most)
        chosen = jnp.where(high == 1.0 * h, both, swapped)
        for c in range(held // LANES):
            value = jnp.where(wanted == 2.0 * c + high, chosen, 0.0)
            wide_ref[h, :, :, c * LANES : (c + 1) * LANES] = value.astype(BF16)
    wide = wide_ref[...].reshape(halves * block * most, held)
    out = jnp.dot(wide, up_ref[...], preferred_element_type=F32)
    out_ref[...] = out.astype(BF16).reshape(out_ref.shape)


def expand_rows(step, names, parts, up, rank, block=8):
    half, most, _ = parts[0].shape
    tiles = names.shape[1] - 1
    held, features = up.shape
    names = names.reshape((2, half) + names.shape[1:])
    delta = pl.pallas_call(
        functools.partial(expand_kernel, step, rank),
        out_shape=pltpu.HBM((2, half, most, features), BF16),
        grid=(half // block,),
        in_specs=[pl.BlockSpec((2, block, 1, TILE, LANES), lambda i: (0, i, tiles, 0, 0))]
        + [pl.BlockSpec((block, most, LANES), lambda i: (i, 0, 0))] * len(parts)
        + [pl.BlockSpec((held, features), lambda i: (0, 0))],
        out_specs=pl.BlockSpec((2, block, most, features), lambda i: (0, i, 0, 0)),
        scratch_shapes=[pltpu.VMEM((2, block, most, held), BF16)],
        compiler_params=pltpu.CompilerParams(vmem_limit_bytes=VMEM),
        cost_estimate=pl.CostEstimate(
            flops=4 * half * most * held * features,
            bytes_accessed=2 * (5 * half * most * LANES + up.size + 2 * half * most * features),
            transcendentals=0,
        ),
        name="expand",
    )(names, *parts, up)
    return delta.reshape(2 * half, most, features)


def shares_kernel(order_ref, tokens_ref, weight_ref, out_ref):
    out_ref[0] = jnp.dot(tokens_ref[...], weight_ref[...], preferred_element_type=F32)


def base_shares(flat_tokens, query_weight, distances):
    size = lax.axis_size("tp")
    rows, width = flat_tokens.shape
    columns = query_weight.shape[1] // size
    order = lax.rem(lax.axis_index("tp") + jnp.array(distances, jnp.int32), size)
    amount = len(distances)
    return pl.pallas_call(
        shares_kernel,
        out_shape=jax.ShapeDtypeStruct((amount, rows, columns), F32),
        grid_spec=pltpu.PrefetchScalarGridSpec(
            num_scalar_prefetch=1,
            grid=(amount,),
            in_specs=[
                pl.BlockSpec((rows, width), lambda k, order: (0, 0)),
                pl.BlockSpec((width, columns), lambda k, order: (0, order[k])),
            ],
            out_specs=pl.BlockSpec((1, rows, columns), lambda k, order: (k, 0, 0)),
        ),
        compiler_params=pltpu.CompilerParams(vmem_limit_bytes=VMEM),
        cost_estimate=pl.CostEstimate(
            flops=2 * rows * width * columns * amount,
            bytes_accessed=2 * width * columns * amount + 4 * rows * columns * amount,
            transcendentals=0,
        ),
        name="shares",
    )(order, flat_tokens, query_weight)


def first_sums_kernel(shares_ref, top_ref, low_ref, right_ref, left_ref):
    middle = top_ref.shape[0]
    right_ref[:middle] = (shares_ref[0, :middle] + top_ref[...].astype(F32)).astype(BF16)
    right_ref[middle:] = shares_ref[0, middle:].astype(BF16)
    left_ref[:middle] = shares_ref[1, :middle].astype(BF16)
    left_ref[middle:] = (shares_ref[1, middle:] + low_ref[...].astype(F32)).astype(BF16)


def first_sums(shares, top, low):
    _, rows, columns = shares.shape
    out = jax.ShapeDtypeStruct((rows, columns), BF16)
    return pl.pallas_call(
        first_sums_kernel,
        out_shape=(out, out),
        compiler_params=pltpu.CompilerParams(vmem_limit_bytes=VMEM),
        cost_estimate=pl.CostEstimate(
            flops=2 * rows * columns, bytes_accessed=14 * rows * columns, transcendentals=0
        ),
        name="first_sums",
    )(shares, top, low)


def join_kernel(spread_ref, back_ref, base_ref, earlier_ref, out_ref):
    groups, most, features = back_ref.shape
    back = back_ref[...].reshape(groups * most, features)
    delta = jnp.dot(spread_ref[...], back, preferred_element_type=F32)
    out_ref[0] = (base_ref[...] + delta).astype(BF16)


def join(step, spread, back, base, earlier):
    rows, places = spread.shape
    groups, most, features = back.shape
    return pl.pallas_call(
        join_kernel,
        out_shape=jax.ShapeDtypeStruct(earlier.shape, BF16),
        grid=(1,),
        in_specs=[
            pl.BlockSpec((rows, places), lambda i: (0, 0)),
            pl.BlockSpec((groups, most, features), lambda i: (0, 0, 0)),
            pl.BlockSpec((rows, features), lambda i: (0, 0)),
            pl.BlockSpec(memory_space=pl.ANY),
        ],
        out_specs=pl.BlockSpec((1, rows, features), lambda i: (step, 0, 0)),
        input_output_aliases={3: 0},
        compiler_params=pltpu.CompilerParams(vmem_limit_bytes=VMEM),
        cost_estimate=pl.CostEstimate(
            flops=2 * rows * places * features,
            bytes_accessed=2 * (spread.size + back.size) + 6 * base.size,
            transcendentals=0,
        ),
        name="join",
    )(spread, back, base, earlier)


def parts_over_tp(value):
    size = lax.axis_size("tp")
    assert size == 8

    def fetch(value, ahead):
        return lax.ppermute(value, "tp", [((i + ahead) % size, i) for i in range(size)])

    after, before = fetch(value, 1), fetch(value, -1)
    two = value.astype(F32) + after.astype(F32)
    three = two + before.astype(F32)
    return value, after, before, fetch(three.astype(BF16), 3), fetch(two.astype(BF16), -3)


def body(tokens, query_weight, down_weight, up_weight, requests, row_slot_index):
    count = lax.axis_size("pool")
    size = lax.axis_size("tp")
    steps, rows, width = tokens.shape
    most = 4 * rows // count
    adapters, rank, _ = down_weight.shape
    features = up_weight.shape[-1]
    middle = steps * rows // 2
    right = [(i, (i + 1) % size) for i in range(size)]
    left = [(i, (i - 1) % size) for i in range(size)]

    def swap(value):
        return lax.all_to_all(value, "pool", split_axis=0, concat_axis=0, tiled=True)

    asked = requests[:, 0, :]
    sent = pack(0, asked, row_slot_index, tokens, most)
    sent, late_tokens, late_slots = lax.optimization_barrier((sent, tokens, row_slot_index))
    x = [swap(sent)]
    sent = pack(1, asked, late_slots, late_tokens, most)

    late_tokens = late_tokens.reshape(steps * rows, width)
    far = size // 2
    far_weight = pltpu.with_memory_space_constraint(query_weight, pltpu.HBM)
    farthest = base_shares(late_tokens, far_weight, [far])[0].astype(BF16)
    top = lax.ppermute(farthest[:middle], "tp", right)
    low = lax.ppermute(farthest[middle:], "tp", left)
    late_tokens, _ = lax.optimization_barrier((late_tokens, farthest))
    near = [d for ahead in range(far - 2, 0, -1) for d in (ahead, size - ahead)] + [0]
    first = base_shares(late_tokens, query_weight, [far - 1, far + 1])
    late_tokens, first = lax.optimization_barrier((late_tokens, first))
    going_right, going_left = first_sums(first, top, low)
    late_tokens, _ = lax.optimization_barrier((late_tokens, going_right))
    shares = base_shares(late_tokens, query_weight, near)
    for hop in range(far - 2):
        going_right = lax.ppermute(going_right, "tp", right).astype(F32) + shares[2 * hop]
        going_left = lax.ppermute(going_left, "tp", left).astype(F32) + shares[2 * hop + 1]
        going_right, going_left = going_right.astype(BF16), going_left.astype(BF16)
        if hop == 0:
            sent, going_right, going_left = lax.optimization_barrier((sent, going_right, going_left))
            x.append(swap(sent))

    down = down_weight.reshape(adapters * rank, width)
    down = pltpu.with_memory_space_constraint(down, pltpu.HBM)
    up = up_weight.reshape(adapters * rank, features)
    names = x[0]
    back = []
    for t in range(steps):
        parts = parts_over_tp(shrink_rows(t, names, x[t], down, most, rank))
        delta = expand_rows(t, names, parts, up, rank)
        if t == steps - 1:
            delta, going_right, going_left = lax.optimization_barrier((delta, going_right, going_left))
        back.append(swap(delta))
    from_left = lax.ppermute(going_right, "tp", right).astype(F32)
    from_right = lax.ppermute(going_left, "tp", left).astype(F32)
    base = (shares[-1] + from_left + from_right).reshape(steps, rows, features)

    slots = late_slots[:, 0, :]
    before = slots[:, None, :] < jnp.arange(count, dtype=jnp.int32)[None, :, None]
    start = jnp.minimum(jnp.sum(before.astype(jnp.int32), axis=2), rows - most)
    mine = slots[:, :, None] == jnp.arange(count, dtype=jnp.int32)[None, None, :]
    own_start = jnp.sum(jnp.where(mine, start[:, None, :], 0), axis=2)
    place = slots * most + jnp.arange(rows, dtype=jnp.int32)[None, :] - own_start
    spread = (place[:, :, None] == jnp.arange(count * most, dtype=jnp.int32)[None, None, :]).astype(BF16)
    out = jnp.zeros((steps, rows, features), BF16)
    for t in range(steps):
        out = join(t, spread[t], back[t], base[t], out)
    return out


def solution(mesh):
    placed = (
        P(None, "pool", "tp"),
        P("tp", None),
        P("pool", None, "tp"),
        P("pool", None, "tp"),
        P(None, "pool", None),
        P(None, "pool", None),
    )
    return jax.shard_map(
        body, mesh=mesh, in_specs=placed, out_specs=P(None, "pool", "tp"), check_vma=False
    )
```

```python
import functools

import jax
import jax.numpy as jnp
from jax import lax
from jax.experimental import pallas as pl
from jax.experimental.pallas import tpu as pltpu
from jax.sharding import PartitionSpec as P

BF16 = jnp.bfloat16
F32 = jnp.float32
LANES = 128
TILE = 16
VMEM = 18 << 20
FULL = 62 << 20


def pack_kernel(step, asked_ref, slots_ref, tokens_ref, out_ref):
    rows, width = tokens_ref.shape[1:]
    block = out_ref.shape[0]
    across = width // LANES
    most = out_ref.shape[1] // across * TILE
    first = pl.program_id(0) * block
    shape = (block, most, rows)
    slot = lax.broadcasted_iota(jnp.int32, shape, 0) + first
    ahead = lax.broadcasted_iota(jnp.int32, shape, 1)
    position = lax.broadcasted_iota(jnp.int32, shape, 2)
    held = jnp.broadcast_to(slots_ref[0].reshape(1, 1, rows), shape)
    before = jnp.where(held < slot, 1.0, 0.0)
    start = jnp.minimum(jnp.sum(before, axis=2, keepdims=True).astype(jnp.int32), rows - most)
    pick = jnp.where(position == start + ahead, 1.0, 0.0).astype(BF16)
    value = jnp.dot(pick.reshape(block * most, rows), tokens_ref[0], preferred_element_type=F32)
    value = value.astype(BF16).reshape(block, most // TILE, TILE, width)
    for down in range(most // TILE):
        for c in range(across):
            out_ref[:, down * across + c] = value[:, down, :, c * LANES : (c + 1) * LANES]
    if step == 0:
        line = lax.broadcasted_iota(jnp.int32, (TILE, LANES), 0)
        for s in range(block):
            names = jnp.where(line < TILE // 2, asked_ref[0, first + s], asked_ref[1, first + s])
            out_ref[s, most // TILE * across] = names.astype(F32).astype(BF16)


def pack(step, asked, slots, tokens, most, block=16):
    _, rows, width = tokens.shape
    count = asked.shape[1]
    tiles = (most // TILE) * (width // LANES) + (1 if step == 0 else 0)
    return pl.pallas_call(
        functools.partial(pack_kernel, step),
        out_shape=jax.ShapeDtypeStruct((count, tiles, TILE, LANES), BF16),
        grid_spec=pltpu.PrefetchScalarGridSpec(
            num_scalar_prefetch=1,
            grid=(count // block,),
            in_specs=[
                pl.BlockSpec((1, 1, rows), lambda i, asked: (step, 0, 0)),
                pl.BlockSpec((1, rows, width), lambda i, asked: (step, 0, 0)),
            ],
            out_specs=pl.BlockSpec((block, tiles, TILE, LANES), lambda i, asked: (i, 0, 0, 0)),
        ),
        compiler_params=pltpu.CompilerParams(vmem_limit_bytes=FULL if step == 0 else VMEM),
        cost_estimate=pl.CostEstimate(
            flops=2 * count * most * rows * width,
            bytes_accessed=2 * (rows * width + count * tiles * TILE * LANES),
            transcendentals=0,
        ),
        name="pack",
    )(asked, slots, tokens)


def named(names_ref, step, half, block, most):
    line = step * (TILE // 2)
    return jnp.broadcast_to(
        names_ref[half, :, 0].astype(F32)[:, line : line + 1, :], (block, most, LANES)
    )


def shrink_kernel(step, rank, names_ref, x_ref, down_ref, out_ref, rows_ref, acc_ref):
    halves, block, most, held = acc_ref.shape
    width = rows_ref.shape[-1]
    across = width // LANES
    for d in range(rows_ref.shape[2]):
        for c in range(across):
            rows_ref[:, :, d, :, c * LANES : (c + 1) * LANES] = x_ref[:, :, d * across + c]
    acc = lax.dot_general(
        rows_ref[...].reshape(halves * block * most, width),
        down_ref[...],
        (((1,), (1,)), ((), ())),
        preferred_element_type=F32,
    )
    acc_ref[...] = acc.reshape(acc_ref.shape)
    lane = lax.broadcasted_iota(jnp.int32, (block * most, LANES), 1)
    parts = []
    for h in range(halves):
        wanted = named(names_ref, step, h, block, most)
        value = jnp.zeros((block, most, LANES), F32)
        odd = jnp.zeros((block, most, LANES), F32)
        for c in range(held // LANES):
            here = acc_ref[h, :, :, c * LANES : (c + 1) * LANES]
            value = jnp.where((wanted == 2.0 * c) | (wanted == 2.0 * c + 1.0), here, value)
            odd = jnp.where(wanted == 2.0 * c + 1.0, 1.0, odd)
        value = value.reshape(block * most, LANES)
        odd = odd.reshape(block * most, LANES)
        parts.append(jnp.where(odd == 1.0 * h, value, pltpu.roll(value, rank, 1)))
    out = jnp.where(lane < rank, parts[0], parts[1])
    out_ref[...] = out.astype(BF16).reshape(out_ref.shape)


def shrink_rows(step, names, x, down, most, rank, block=8):
    half = x.shape[0] // 2
    held, width = down.shape
    tiles = (most // TILE) * (width // LANES)
    names = names.reshape((2, half) + names.shape[1:])
    x = x.reshape((2, half) + x.shape[1:])
    return pl.pallas_call(
        functools.partial(shrink_kernel, step, rank),
        out_shape=jax.ShapeDtypeStruct((half, most, LANES), BF16),
        grid=(half // block,),
        in_specs=[
            pl.BlockSpec((2, block, 1, TILE, LANES), lambda i: (0, i, tiles, 0, 0)),
            pl.BlockSpec((2, block, tiles, TILE, LANES), lambda i: (0, i, 0, 0, 0)),
            pl.BlockSpec((held, width), lambda i: (0, 0)),
        ],
        out_specs=pl.BlockSpec((block, most, LANES), lambda i: (i, 0, 0)),
        scratch_shapes=[
            pltpu.VMEM((2, block, most // TILE, TILE, width), BF16),
            pltpu.VMEM((2, block, most, held), F32),
        ],
        compiler_params=pltpu.CompilerParams(vmem_limit_bytes=VMEM),
        cost_estimate=pl.CostEstimate(
            flops=4 * half * most * width * held,
            bytes_accessed=2 * (x.size + down.size),
            transcendentals=0,
        ),
        name="shrink",
    )(names, x, down)


def expand_kernel(step, rank, names_ref, a_ref, b_ref, c_ref, d_ref, e_ref, up_ref, out_ref, wide_ref):
    halves, block, most, held = wide_ref.shape
    both = a_ref[...].astype(F32)
    for ref in (b_ref, c_ref, d_ref, e_ref):
        both = both + ref[...].astype(F32)
    swapped = pltpu.roll(both.reshape(block * most, LANES), rank, 1).reshape(block, most, LANES)
    high = jnp.where(lax.broadcasted_iota(jnp.int32, (block, most, LANES), 2) < rank, 0.0, 1.0)
    for h in range(halves):
        wanted = named(names_ref, step, h, block, most)
        chosen = jnp.where(high == 1.0 * h, both, swapped)
        for c in range(held // LANES):
            value = jnp.where(wanted == 2.0 * c + high, chosen, 0.0)
            wide_ref[h, :, :, c * LANES : (c + 1) * LANES] = value.astype(BF16)
    wide = wide_ref[...].reshape(halves * block * most, held)
    out = jnp.dot(wide, up_ref[...], preferred_element_type=F32)
    out_ref[...] = out.astype(BF16).reshape(out_ref.shape)


def expand_rows(step, names, parts, up, rank, block=8):
    half, most, _ = parts[0].shape
    tiles = names.shape[1] - 1
    held, features = up.shape
    names = names.reshape((2, half) + names.shape[1:])
    delta = pl.pallas_call(
        functools.partial(expand_kernel, step, rank),
        out_shape=pltpu.HBM((2, half, most, features), BF16),
        grid=(half // block,),
        in_specs=[pl.BlockSpec((2, block, 1, TILE, LANES), lambda i: (0, i, tiles, 0, 0))]
        + [pl.BlockSpec((block, most, LANES), lambda i: (i, 0, 0))] * len(parts)
        + [pl.BlockSpec((held, features), lambda i: (0, 0))],
        out_specs=pl.BlockSpec((2, block, most, features), lambda i: (0, i, 0, 0)),
        scratch_shapes=[pltpu.VMEM((2, block, most, held), BF16)],
        compiler_params=pltpu.CompilerParams(vmem_limit_bytes=VMEM),
        cost_estimate=pl.CostEstimate(
            flops=4 * half * most * held * features,
            bytes_accessed=2 * (5 * half * most * LANES + up.size + 2 * half * most * features),
            transcendentals=0,
        ),
        name="expand",
    )(names, *parts, up)
    return delta.reshape(2 * half, most, features)


def shares_kernel(order_ref, tokens_ref, weight_ref, out_ref):
    out_ref[0] = jnp.dot(tokens_ref[...], weight_ref[...], preferred_element_type=F32)


def base_shares(flat_tokens, query_weight, distances):
    size = lax.axis_size("tp")
    rows, width = flat_tokens.shape
    columns = query_weight.shape[1] // size
    order = lax.rem(lax.axis_index("tp") + jnp.array(distances, jnp.int32), size)
    amount = len(distances)
    return pl.pallas_call(
        shares_kernel,
        out_shape=jax.ShapeDtypeStruct((amount, rows, columns), F32),
        grid_spec=pltpu.PrefetchScalarGridSpec(
            num_scalar_prefetch=1,
            grid=(amount,),
            in_specs=[
                pl.BlockSpec((rows, width), lambda k, order: (0, 0)),
                pl.BlockSpec((width, columns), lambda k, order: (0, order[k])),
            ],
            out_specs=pl.BlockSpec((1, rows, columns), lambda k, order: (k, 0, 0)),
        ),
        compiler_params=pltpu.CompilerParams(vmem_limit_bytes=VMEM),
        cost_estimate=pl.CostEstimate(
            flops=2 * rows * width * columns * amount,
            bytes_accessed=2 * width * columns * amount + 4 * rows * columns * amount,
            transcendentals=0,
        ),
        name="shares",
    )(order, flat_tokens, query_weight)


def first_sums_kernel(shares_ref, top_ref, low_ref, right_ref, left_ref):
    middle = top_ref.shape[0]
    right_ref[:middle] = (shares_ref[0, :middle] + top_ref[...].astype(F32)).astype(BF16)
    right_ref[middle:] = shares_ref[0, middle:].astype(BF16)
    left_ref[:middle] = shares_ref[1, :middle].astype(BF16)
    left_ref[middle:] = (shares_ref[1, middle:] + low_ref[...].astype(F32)).astype(BF16)


def first_sums(shares, top, low):
    _, rows, columns = shares.shape
    out = jax.ShapeDtypeStruct((rows, columns), BF16)
    return pl.pallas_call(
        first_sums_kernel,
        out_shape=(out, out),
        compiler_params=pltpu.CompilerParams(vmem_limit_bytes=VMEM),
        cost_estimate=pl.CostEstimate(
            flops=2 * rows * columns, bytes_accessed=14 * rows * columns, transcendentals=0
        ),
        name="first_sums",
    )(shares, top, low)


def join_kernel(spread_ref, back_ref, base_ref, earlier_ref, out_ref):
    groups, most, features = back_ref.shape
    back = back_ref[...].reshape(groups * most, features)
    delta = jnp.dot(spread_ref[...], back, preferred_element_type=F32)
    out_ref[0] = (base_ref[...] + delta).astype(BF16)


def join(step, spread, back, base, earlier):
    rows, places = spread.shape
    groups, most, features = back.shape
    return pl.pallas_call(
        join_kernel,
        out_shape=jax.ShapeDtypeStruct(earlier.shape, BF16),
        grid=(1,),
        in_specs=[
            pl.BlockSpec((rows, places), lambda i: (0, 0)),
            pl.BlockSpec((groups, most, features), lambda i: (0, 0, 0)),
            pl.BlockSpec((rows, features), lambda i: (0, 0)),
            pl.BlockSpec(memory_space=pl.ANY),
        ],
        out_specs=pl.BlockSpec((1, rows, features), lambda i: (step, 0, 0)),
        input_output_aliases={3: 0},
        compiler_params=pltpu.CompilerParams(vmem_limit_bytes=VMEM),
        cost_estimate=pl.CostEstimate(
            flops=2 * rows * places * features,
            bytes_accessed=2 * (spread.size + back.size) + 6 * base.size,
            transcendentals=0,
        ),
        name="join",
    )(spread, back, base, earlier)


def parts_over_tp(value):
    size = lax.axis_size("tp")
    assert size == 8

    def fetch(value, ahead):
        return lax.ppermute(value, "tp", [((i + ahead) % size, i) for i in range(size)])

    after, before = fetch(value, 1), fetch(value, -1)
    two = value.astype(F32) + after.astype(F32)
    three = two + before.astype(F32)
    return value, after, before, fetch(three.astype(BF16), 3), fetch(two.astype(BF16), -3)


def body(tokens, query_weight, down_weight, up_weight, requests, row_slot_index):
    count = lax.axis_size("pool")
    size = lax.axis_size("tp")
    steps, rows, width = tokens.shape
    most = 4 * rows // count
    adapters, rank, _ = down_weight.shape
    features = up_weight.shape[-1]
    middle = steps * rows // 2
    right = [(i, (i + 1) % size) for i in range(size)]
    left = [(i, (i - 1) % size) for i in range(size)]

    def swap(value):
        return lax.all_to_all(value, "pool", split_axis=0, concat_axis=0, tiled=True)

    asked = requests[:, 0, :]
    sent = pack(0, asked, row_slot_index, tokens, most)
    sent, late_tokens, late_slots = lax.optimization_barrier((sent, tokens, row_slot_index))
    x = [swap(sent)]
    sent = pack(1, asked, late_slots, late_tokens, most)

    late_tokens = late_tokens.reshape(steps * rows, width)
    far = size // 2
    far_weight = pltpu.with_memory_space_constraint(query_weight, pltpu.HBM)
    farthest = base_shares(late_tokens, far_weight, [far])[0].astype(BF16)
    top = lax.ppermute(farthest[:middle], "tp", right)
    low = lax.ppermute(farthest[middle:], "tp", left)
    late_tokens, _ = lax.optimization_barrier((late_tokens, farthest))
    near = [d for ahead in range(far - 2, 0, -1) for d in (ahead, size - ahead)] + [0]
    first = base_shares(late_tokens, query_weight, [far - 1, far + 1])
    late_tokens, first = lax.optimization_barrier((late_tokens, first))
    going_right, going_left = first_sums(first, top, low)
    late_tokens, _ = lax.optimization_barrier((late_tokens, going_right))
    shares = base_shares(late_tokens, query_weight, near)
    down = pltpu.with_memory_space_constraint(down_weight.reshape(adapters * rank, width), pltpu.HBM)
    going_right = lax.ppermute(going_right, "tp", right).astype(F32) + shares[0]
    going_left = lax.ppermute(going_left, "tp", left).astype(F32) + shares[1]
    going_right, going_left = going_right.astype(BF16), going_left.astype(BF16)
    names = x[0]
    shrunk = shrink_rows(0, names, x[0], down, most, rank)
    sent, going_right, going_left = lax.optimization_barrier((sent, going_right, going_left))
    x.append(swap(sent))

    up = up_weight.reshape(adapters * rank, features)
    back = []
    delta = expand_rows(0, names, parts_over_tp(shrunk), up, rank)
    going_right = lax.ppermute(going_right, "tp", right)
    going_left = lax.ppermute(going_left, "tp", left)
    shrunk = shrink_rows(1, names, x[1], down, most, rank)
    delta, shrunk = lax.optimization_barrier((delta, shrunk))
    back.append(swap(delta))
    delta = expand_rows(1, names, parts_over_tp(shrunk), up, rank)
    going_right = (going_right.astype(F32) + shares[2]).astype(BF16)
    going_left = (going_left.astype(F32) + shares[3]).astype(BF16)
    delta, going_right, going_left = lax.optimization_barrier((delta, going_right, going_left))
    back.append(swap(delta))
    from_left = lax.ppermute(going_right, "tp", right).astype(F32)
    from_right = lax.ppermute(going_left, "tp", left).astype(F32)
    base = (shares[-1] + from_left + from_right).reshape(steps, rows, features)

    slots = late_slots[:, 0, :]
    before = slots[:, None, :] < jnp.arange(count, dtype=jnp.int32)[None, :, None]
    start = jnp.minimum(jnp.sum(before.astype(jnp.int32), axis=2), rows - most)
    mine = slots[:, :, None] == jnp.arange(count, dtype=jnp.int32)[None, None, :]
    own_start = jnp.sum(jnp.where(mine, start[:, None, :], 0), axis=2)
    place = slots * most + jnp.arange(rows, dtype=jnp.int32)[None, :] - own_start
    spread = (place[:, :, None] == jnp.arange(count * most, dtype=jnp.int32)[None, None, :]).astype(BF16)
    out = jnp.zeros((steps, rows, features), BF16)
    for t in range(steps):
        out = join(t, spread[t], back[t], base[t], out)
    return out


def solution(mesh):
    placed = (
        P(None, "pool", "tp"),
        P("tp", None),
        P("pool", None, "tp"),
        P("pool", None, "tp"),
        P(None, "pool", None),
        P(None, "pool", None),
    )
    return jax.shard_map(
        body, mesh=mesh, in_specs=placed, out_specs=P(None, "pool", "tp"), check_vma=False
    )
```

```python
import functools

import jax
import jax.numpy as jnp
from jax import lax
from jax.experimental import pallas as pl
from jax.experimental.pallas import tpu as pltpu
from jax.sharding import PartitionSpec as P

BF16 = jnp.bfloat16
F32 = jnp.float32
LANES = 128
TILE = 16
VMEM = 18 << 20
FULL = 62 << 20


def pack_kernel(step, asked_ref, slots_ref, tokens_ref, out_ref):
    rows, width = tokens_ref.shape[1:]
    block = out_ref.shape[0]
    across = width // LANES
    most = out_ref.shape[1] // across * TILE
    first = pl.program_id(0) * block
    shape = (block, most, rows)
    slot = lax.broadcasted_iota(jnp.int32, shape, 0) + first
    ahead = lax.broadcasted_iota(jnp.int32, shape, 1)
    position = lax.broadcasted_iota(jnp.int32, shape, 2)
    held = jnp.broadcast_to(slots_ref[0].reshape(1, 1, rows), shape)
    before = jnp.where(held < slot, 1.0, 0.0)
    start = jnp.minimum(jnp.sum(before, axis=2, keepdims=True).astype(jnp.int32), rows - most)
    pick = jnp.where(position == start + ahead, 1.0, 0.0).astype(BF16)
    value = jnp.dot(pick.reshape(block * most, rows), tokens_ref[0], preferred_element_type=F32)
    value = value.astype(BF16).reshape(block, most // TILE, TILE, width)
    for down in range(most // TILE):
        for c in range(across):
            out_ref[:, down * across + c] = value[:, down, :, c * LANES : (c + 1) * LANES]
    if step == 0:
        shape = (block, TILE, asked_ref.shape[1])
        here = lax.broadcasted_iota(jnp.int32, shape, 2) == lax.broadcasted_iota(jnp.int32, shape, 0) + first
        line = lax.broadcasted_iota(jnp.int32, shape, 1)
        asked = jnp.where(
            line < TILE // 2,
            jnp.broadcast_to(asked_ref[0:1, :].reshape(1, 1, -1), shape),
            jnp.broadcast_to(asked_ref[1:2, :].reshape(1, 1, -1), shape),
        )
        names = jnp.sum(jnp.where(here, asked.astype(F32), 0.0), axis=2, keepdims=True)
        names = jnp.broadcast_to(names, (block, TILE, LANES))
        out_ref[:, most // TILE * across] = names.astype(BF16)


def pack(step, asked, slots, tokens, most, block=16):
    _, rows, width = tokens.shape
    count = asked.shape[1]
    tiles = (most // TILE) * (width // LANES) + (1 if step == 0 else 0)
    return pl.pallas_call(
        functools.partial(pack_kernel, step),
        out_shape=jax.ShapeDtypeStruct((count, tiles, TILE, LANES), BF16),
        grid=(count // block,),
        in_specs=[
            pl.BlockSpec(asked.shape, lambda i: (0, 0)),
            pl.BlockSpec((1, 1, rows), lambda i: (step, 0, 0)),
            pl.BlockSpec((1, rows, width), lambda i: (step, 0, 0)),
        ],
        out_specs=pl.BlockSpec((block, tiles, TILE, LANES), lambda i: (i, 0, 0, 0)),
        compiler_params=pltpu.CompilerParams(vmem_limit_bytes=FULL if step == 0 else VMEM),
        cost_estimate=pl.CostEstimate(
            flops=2 * count * most * rows * width,
            bytes_accessed=2 * (rows * width + count * tiles * TILE * LANES),
            transcendentals=0,
        ),
        name="pack",
    )(asked, slots, tokens)


def named(names_ref, step, half, block, most):
    line = step * (TILE // 2)
    return jnp.broadcast_to(
        names_ref[half, :, 0].astype(F32)[:, line : line + 1, :], (block, most, LANES)
    )


def shrink_kernel(step, rank, names_ref, x_ref, down_ref, out_ref, rows_ref, acc_ref):
    halves, block, most, held = acc_ref.shape
    width = rows_ref.shape[-1]
    across = width // LANES
    for d in range(rows_ref.shape[2]):
        for c in range(across):
            rows_ref[:, :, d, :, c * LANES : (c + 1) * LANES] = x_ref[:, :, d * across + c]
    acc = lax.dot_general(
        rows_ref[...].reshape(halves * block * most, width),
        down_ref[...],
        (((1,), (1,)), ((), ())),
        preferred_element_type=F32,
    )
    acc_ref[...] = acc.reshape(acc_ref.shape)
    lane = lax.broadcasted_iota(jnp.int32, (block * most, LANES), 1)
    parts = []
    for h in range(halves):
        wanted = named(names_ref, step, h, block, most)
        pair = jnp.floor(wanted * 0.5)
        odd = wanted - 2.0 * pair
        value = acc_ref[h, :, :, :LANES]
        for c in range(1, held // LANES):
            value = jnp.where(pair == 1.0 * c, acc_ref[h, :, :, c * LANES : (c + 1) * LANES], value)
        value = value.reshape(block * most, LANES)
        odd = odd.reshape(block * most, LANES)
        parts.append(jnp.where(odd == 1.0 * h, value, pltpu.roll(value, rank, 1)))
    out = jnp.where(lane < rank, parts[0], parts[1])
    out_ref[...] = out.astype(BF16).reshape(out_ref.shape)


def shrink_rows(step, names, x, down, most, rank, block=8):
    half = x.shape[0] // 2
    held, width = down.shape
    tiles = (most // TILE) * (width // LANES)
    names = names.reshape((2, half) + names.shape[1:])
    x = x.reshape((2, half) + x.shape[1:])
    return pl.pallas_call(
        functools.partial(shrink_kernel, step, rank),
        out_shape=jax.ShapeDtypeStruct((half, most, LANES), BF16),
        grid=(half // block,),
        in_specs=[
            pl.BlockSpec((2, block, 1, TILE, LANES), lambda i: (0, i, tiles, 0, 0)),
            pl.BlockSpec((2, block, tiles, TILE, LANES), lambda i: (0, i, 0, 0, 0)),
            pl.BlockSpec((held, width), lambda i: (0, 0)),
        ],
        out_specs=pl.BlockSpec((block, most, LANES), lambda i: (i, 0, 0)),
        scratch_shapes=[
            pltpu.VMEM((2, block, most // TILE, TILE, width), BF16),
            pltpu.VMEM((2, block, most, held), F32),
        ],
        compiler_params=pltpu.CompilerParams(vmem_limit_bytes=VMEM),
        cost_estimate=pl.CostEstimate(
            flops=4 * half * most * width * held,
            bytes_accessed=2 * (x.size + down.size),
            transcendentals=0,
        ),
        name="shrink",
    )(names, x, down)


def expand_kernel(step, rank, names_ref, a_ref, b_ref, c_ref, d_ref, e_ref, up_ref, out_ref, wide_ref):
    halves, block, most, held = wide_ref.shape
    both = a_ref[...].astype(F32)
    for ref in (b_ref, c_ref, d_ref, e_ref):
        both = both + ref[...].astype(F32)
    swapped = pltpu.roll(both.reshape(block * most, LANES), rank, 1).reshape(block, most, LANES)
    high = jnp.where(lax.broadcasted_iota(jnp.int32, (block, most, LANES), 2) < rank, 0.0, 1.0)
    for h in range(halves):
        wanted = named(names_ref, step, h, block, most)
        chosen = jnp.where(high == 1.0 * h, both, swapped)
        place = (wanted - high) * 0.5
        for c in range(held // LANES):
            value = jnp.where(place == 1.0 * c, chosen, 0.0)
            wide_ref[h, :, :, c * LANES : (c + 1) * LANES] = value.astype(BF16)
    wide = wide_ref[...].reshape(halves * block * most, held)
    out = jnp.dot(wide, up_ref[...], preferred_element_type=F32)
    out_ref[...] = out.astype(BF16).reshape(out_ref.shape)


def expand_rows(step, names, parts, up, rank, block=8):
    half, most, _ = parts[0].shape
    tiles = names.shape[1] - 1
    held, features = up.shape
    names = names.reshape((2, half) + names.shape[1:])
    delta = pl.pallas_call(
        functools.partial(expand_kernel, step, rank),
        out_shape=pltpu.HBM((2, half, most, features), BF16),
        grid=(half // block,),
        in_specs=[pl.BlockSpec((2, block, 1, TILE, LANES), lambda i: (0, i, tiles, 0, 0))]
        + [pl.BlockSpec((block, most, LANES), lambda i: (i, 0, 0))] * len(parts)
        + [pl.BlockSpec((held, features), lambda i: (0, 0))],
        out_specs=pl.BlockSpec((2, block, most, features), lambda i: (0, i, 0, 0)),
        scratch_shapes=[pltpu.VMEM((2, block, most, held), BF16)],
        compiler_params=pltpu.CompilerParams(vmem_limit_bytes=VMEM),
        cost_estimate=pl.CostEstimate(
            flops=4 * half * most * held * features,
            bytes_accessed=2 * (5 * half * most * LANES + up.size + 2 * half * most * features),
            transcendentals=0,
        ),
        name="expand",
    )(names, *parts, up)
    return delta.reshape(2 * half, most, features)


def shares_kernel(order_ref, tokens_ref, weight_ref, out_ref):
    out_ref[0] = jnp.dot(tokens_ref[...], weight_ref[...], preferred_element_type=F32)


def base_shares(flat_tokens, query_weight, distances):
    size = lax.axis_size("tp")
    rows, width = flat_tokens.shape
    columns = query_weight.shape[1] // size
    order = lax.rem(lax.axis_index("tp") + jnp.array(distances, jnp.int32), size)
    amount = len(distances)
    return pl.pallas_call(
        shares_kernel,
        out_shape=jax.ShapeDtypeStruct((amount, rows, columns), F32),
        grid_spec=pltpu.PrefetchScalarGridSpec(
            num_scalar_prefetch=1,
            grid=(amount,),
            in_specs=[
                pl.BlockSpec((rows, width), lambda k, order: (0, 0)),
                pl.BlockSpec((width, columns), lambda k, order: (0, order[k])),
            ],
            out_specs=pl.BlockSpec((1, rows, columns), lambda k, order: (k, 0, 0)),
        ),
        compiler_params=pltpu.CompilerParams(vmem_limit_bytes=VMEM),
        cost_estimate=pl.CostEstimate(
            flops=2 * rows * width * columns * amount,
            bytes_accessed=2 * width * columns * amount + 4 * rows * columns * amount,
            transcendentals=0,
        ),
        name="shares",
    )(order, flat_tokens, query_weight)


def first_sums_kernel(shares_ref, top_ref, low_ref, right_ref, left_ref):
    middle = top_ref.shape[0]
    right_ref[:middle] = (shares_ref[0, :middle] + top_ref[...].astype(F32)).astype(BF16)
    right_ref[middle:] = shares_ref[0, middle:].astype(BF16)
    left_ref[:middle] = shares_ref[1, :middle].astype(BF16)
    left_ref[middle:] = (shares_ref[1, middle:] + low_ref[...].astype(F32)).astype(BF16)


def first_sums(shares, top, low):
    _, rows, columns = shares.shape
    out = jax.ShapeDtypeStruct((rows, columns), BF16)
    return pl.pallas_call(
        first_sums_kernel,
        out_shape=(out, out),
        compiler_params=pltpu.CompilerParams(vmem_limit_bytes=VMEM),
        cost_estimate=pl.CostEstimate(
            flops=2 * rows * columns, bytes_accessed=14 * rows * columns, transcendentals=0
        ),
        name="first_sums",
    )(shares, top, low)


def join_kernel(spread_ref, back_ref, base_ref, earlier_ref, out_ref):
    groups, most, features = back_ref.shape
    back = back_ref[...].reshape(groups * most, features)
    delta = jnp.dot(spread_ref[...], back, preferred_element_type=F32)
    out_ref[0] = (base_ref[...] + delta).astype(BF16)


def join(step, spread, back, base, earlier):
    rows, places = spread.shape
    groups, most, features = back.shape
    return pl.pallas_call(
        join_kernel,
        out_shape=jax.ShapeDtypeStruct(earlier.shape, BF16),
        grid=(1,),
        in_specs=[
            pl.BlockSpec((rows, places), lambda i: (0, 0)),
            pl.BlockSpec((groups, most, features), lambda i: (0, 0, 0)),
            pl.BlockSpec((rows, features), lambda i: (0, 0)),
            pl.BlockSpec(memory_space=pl.ANY),
        ],
        out_specs=pl.BlockSpec((1, rows, features), lambda i: (step, 0, 0)),
        input_output_aliases={3: 0},
        compiler_params=pltpu.CompilerParams(vmem_limit_bytes=VMEM),
        cost_estimate=pl.CostEstimate(
            flops=2 * rows * places * features,
            bytes_accessed=2 * (spread.size + back.size) + 6 * base.size,
            transcendentals=0,
        ),
        name="join",
    )(spread, back, base, earlier)


def parts_over_tp(value):
    size = lax.axis_size("tp")
    assert size == 8

    def fetch(value, ahead):
        return lax.ppermute(value, "tp", [((i + ahead) % size, i) for i in range(size)])

    after, before = fetch(value, 1), fetch(value, -1)
    two = value.astype(F32) + after.astype(F32)
    three = two + before.astype(F32)
    return value, after, before, fetch(three.astype(BF16), 3), fetch(two.astype(BF16), -3)


def body(tokens, query_weight, down_weight, up_weight, requests, row_slot_index):
    count = lax.axis_size("pool")
    size = lax.axis_size("tp")
    steps, rows, width = tokens.shape
    most = 4 * rows // count
    adapters, rank, _ = down_weight.shape
    features = up_weight.shape[-1]
    middle = steps * rows // 2
    right = [(i, (i + 1) % size) for i in range(size)]
    left = [(i, (i - 1) % size) for i in range(size)]

    def swap(value):
        return lax.all_to_all(value, "pool", split_axis=0, concat_axis=0, tiled=True)

    asked = requests[:, 0, :]
    sent = pack(0, asked, row_slot_index, tokens, most)
    sent, late_tokens, late_slots = lax.optimization_barrier((sent, tokens, row_slot_index))
    x = [swap(sent)]
    sent = pack(1, asked, late_slots, late_tokens, most)

    late_tokens = late_tokens.reshape(steps * rows, width)
    far = size // 2
    far_weight = pltpu.with_memory_space_constraint(query_weight, pltpu.HBM)
    farthest = base_shares(late_tokens, far_weight, [far])[0].astype(BF16)
    top = lax.ppermute(farthest[:middle], "tp", right)
    low = lax.ppermute(farthest[middle:], "tp", left)
    late_tokens, _ = lax.optimization_barrier((late_tokens, farthest))
    near = [d for ahead in range(far - 2, 0, -1) for d in (ahead, size - ahead)] + [0]
    first = base_shares(late_tokens, query_weight, [far - 1, far + 1])
    late_tokens, first = lax.optimization_barrier((late_tokens, first))
    going_right, going_left = first_sums(first, top, low)
    late_tokens, _ = lax.optimization_barrier((late_tokens, going_right))
    shares = base_shares(late_tokens, query_weight, near)
    down = pltpu.with_memory_space_constraint(down_weight.reshape(adapters * rank, width), pltpu.HBM)
    going_right = lax.ppermute(going_right, "tp", right)
    going_left = lax.ppermute(going_left, "tp", left)
    names = x[0]
    shrunk = shrink_rows(0, names, x[0], down, most, rank)
    sent, going_right, going_left, shares = lax.optimization_barrier((sent, going_right, going_left, shares))
    x.append(swap(sent))
    going_right = (going_right.astype(F32) + shares[0]).astype(BF16)
    going_left = (going_left.astype(F32) + shares[1]).astype(BF16)

    up = up_weight.reshape(adapters * rank, features)
    back = []
    delta = expand_rows(0, names, parts_over_tp(shrunk), up, rank)
    going_right = lax.ppermute(going_right, "tp", right)
    going_left = lax.ppermute(going_left, "tp", left)
    shrunk = shrink_rows(1, names, x[1], down, most, rank)
    delta, shrunk = lax.optimization_barrier((delta, shrunk))
    back.append(swap(delta))
    delta = expand_rows(1, names, parts_over_tp(shrunk), up, rank)
    going_right = (going_right.astype(F32) + shares[2]).astype(BF16)
    going_left = (going_left.astype(F32) + shares[3]).astype(BF16)
    delta, going_right, going_left = lax.optimization_barrier((delta, going_right, going_left))
    back.append(swap(delta))
    from_left = lax.ppermute(going_right, "tp", right).astype(F32)
    from_right = lax.ppermute(going_left, "tp", left).astype(F32)
    base = (shares[-1] + from_left + from_right).reshape(steps, rows, features)

    slots = late_slots[:, 0, :]
    before = slots[:, None, :] < jnp.arange(count, dtype=jnp.int32)[None, :, None]
    start = jnp.minimum(jnp.sum(before.astype(jnp.int32), axis=2), rows - most)
    mine = slots[:, :, None] == jnp.arange(count, dtype=jnp.int32)[None, None, :]
    own_start = jnp.sum(jnp.where(mine, start[:, None, :], 0), axis=2)
    place = slots * most + jnp.arange(rows, dtype=jnp.int32)[None, :] - own_start
    spread = (place[:, :, None] == jnp.arange(count * most, dtype=jnp.int32)[None, None, :]).astype(BF16)
    out = jnp.zeros((steps, rows, features), BF16)
    for t in range(steps):
        out = join(t, spread[t], back[t], base[t], out)
    return out


def solution(mesh):
    placed = (
        P(None, "pool", "tp"),
        P("tp", None),
        P("pool", None, "tp"),
        P("pool", None, "tp"),
        P(None, "pool", None),
        P(None, "pool", None),
    )
    return jax.shard_map(
        body, mesh=mesh, in_specs=placed, out_specs=P(None, "pool", "tp"), check_vma=False
    )
```

```python
import functools

import jax
import jax.numpy as jnp
from jax import lax
from jax.experimental import pallas as pl
from jax.experimental.pallas import tpu as pltpu
from jax.sharding import PartitionSpec as P

BF16 = jnp.bfloat16
F32 = jnp.float32
LANES = 128
TILE = 16
VMEM = 18 << 20
FULL = 62 << 20


def pack_kernel(step, asked_ref, slots_ref, tokens_ref, out_ref):
    rows, width = tokens_ref.shape[1:]
    block = out_ref.shape[0]
    across = width // LANES
    most = out_ref.shape[1] // across * TILE
    first = pl.program_id(0) * block
    shape = (block, most, rows)
    slot = lax.broadcasted_iota(jnp.int32, shape, 0) + first
    ahead = lax.broadcasted_iota(jnp.int32, shape, 1)
    position = lax.broadcasted_iota(jnp.int32, shape, 2)
    held = jnp.broadcast_to(slots_ref[0].reshape(1, 1, rows), shape)
    before = jnp.where(held < slot, 1.0, 0.0)
    start = jnp.minimum(jnp.sum(before, axis=2, keepdims=True).astype(jnp.int32), rows - most)
    pick = jnp.where(position == start + ahead, 1.0, 0.0).astype(BF16)
    value = jnp.dot(pick.reshape(block * most, rows), tokens_ref[0], preferred_element_type=F32)
    value = value.astype(BF16).reshape(block, most // TILE, TILE, width)
    for down in range(most // TILE):
        for c in range(across):
            out_ref[:, down * across + c] = value[:, down, :, c * LANES : (c + 1) * LANES]
    if step == 0:
        shape = (block, TILE, asked_ref.shape[1])
        here = lax.broadcasted_iota(jnp.int32, shape, 2) == lax.broadcasted_iota(jnp.int32, shape, 0) + first
        line = lax.broadcasted_iota(jnp.int32, shape, 1)
        asked = jnp.where(
            line < TILE // 2,
            jnp.broadcast_to(asked_ref[0:1, :].reshape(1, 1, -1), shape),
            jnp.broadcast_to(asked_ref[1:2, :].reshape(1, 1, -1), shape),
        )
        names = jnp.sum(jnp.where(here, asked.astype(F32), 0.0), axis=2, keepdims=True)
        names = jnp.broadcast_to(names, (block, TILE, LANES))
        out_ref[:, most // TILE * across] = names.astype(BF16)


def pack(step, asked, slots, tokens, most, block=16):
    _, rows, width = tokens.shape
    count = asked.shape[1]
    tiles = (most // TILE) * (width // LANES) + (1 if step == 0 else 0)
    return pl.pallas_call(
        functools.partial(pack_kernel, step),
        out_shape=jax.ShapeDtypeStruct((count, tiles, TILE, LANES), BF16),
        grid=(count // block,),
        in_specs=[
            pl.BlockSpec(asked.shape, lambda i: (0, 0)),
            pl.BlockSpec((1, 1, rows), lambda i: (step, 0, 0)),
            pl.BlockSpec((1, rows, width), lambda i: (step, 0, 0)),
        ],
        out_specs=pl.BlockSpec((block, tiles, TILE, LANES), lambda i: (i, 0, 0, 0)),
        compiler_params=pltpu.CompilerParams(vmem_limit_bytes=FULL if step == 0 else VMEM),
        cost_estimate=pl.CostEstimate(
            flops=2 * count * most * rows * width,
            bytes_accessed=2 * (rows * width + count * tiles * TILE * LANES),
            transcendentals=0,
        ),
        name="pack",
    )(asked, slots, tokens)


def named(names_ref, step, half, block, most):
    line = step * (TILE // 2)
    return jnp.broadcast_to(
        names_ref[half, :, 0].astype(F32)[:, line : line + 1, :], (block, most, LANES)
    )


def shrink_kernel(step, rank, names_ref, x_ref, down_ref, out_ref, rows_ref, acc_ref):
    halves, block, most, held = acc_ref.shape
    width = rows_ref.shape[-1]
    across = width // LANES
    for d in range(rows_ref.shape[2]):
        for c in range(across):
            rows_ref[:, :, d, :, c * LANES : (c + 1) * LANES] = x_ref[:, :, d * across + c]
    acc = lax.dot_general(
        rows_ref[...].reshape(halves * block * most, width),
        down_ref[...],
        (((1,), (1,)), ((), ())),
        preferred_element_type=F32,
    )
    acc_ref[...] = acc.reshape(acc_ref.shape)
    lane = lax.broadcasted_iota(jnp.int32, (block * most, LANES), 1)
    parts = []
    for h in range(halves):
        wanted = named(names_ref, step, h, block, most)
        pair = jnp.floor(wanted * 0.5)
        odd = wanted - 2.0 * pair
        value = acc_ref[h, :, :, :LANES]
        for c in range(1, held // LANES):
            value = jnp.where(pair == 1.0 * c, acc_ref[h, :, :, c * LANES : (c + 1) * LANES], value)
        value = value.reshape(block * most, LANES)
        odd = odd.reshape(block * most, LANES)
        parts.append(jnp.where(odd == 1.0 * h, value, pltpu.roll(value, rank, 1)))
    out = jnp.where(lane < rank, parts[0], parts[1])
    out_ref[...] = out.astype(BF16).reshape(out_ref.shape)


def shrink_rows(step, names, x, down, most, rank, block=8):
    half = x.shape[0] // 2
    held, width = down.shape
    tiles = (most // TILE) * (width // LANES)
    names = names.reshape((2, half) + names.shape[1:])
    x = x.reshape((2, half) + x.shape[1:])
    return pl.pallas_call(
        functools.partial(shrink_kernel, step, rank),
        out_shape=jax.ShapeDtypeStruct((half, most, LANES), BF16),
        grid=(half // block,),
        in_specs=[
            pl.BlockSpec((2, block, 1, TILE, LANES), lambda i: (0, i, tiles, 0, 0)),
            pl.BlockSpec((2, block, tiles, TILE, LANES), lambda i: (0, i, 0, 0, 0)),
            pl.BlockSpec((held, width), lambda i: (0, 0)),
        ],
        out_specs=pl.BlockSpec((block, most, LANES), lambda i: (i, 0, 0)),
        scratch_shapes=[
            pltpu.VMEM((2, block, most // TILE, TILE, width), BF16),
            pltpu.VMEM((2, block, most, held), F32),
        ],
        compiler_params=pltpu.CompilerParams(vmem_limit_bytes=VMEM),
        cost_estimate=pl.CostEstimate(
            flops=4 * half * most * width * held,
            bytes_accessed=2 * (x.size + down.size),
            transcendentals=0,
        ),
        name="shrink",
    )(names, x, down)


def expand_kernel(step, rank, names_ref, a_ref, b_ref, c_ref, d_ref, e_ref, up_ref, out_ref, wide_ref):
    halves, block, most, held = wide_ref.shape
    both = a_ref[...].astype(F32)
    for ref in (b_ref, c_ref, d_ref, e_ref):
        both = both + ref[...].astype(F32)
    swapped = pltpu.roll(both.reshape(block * most, LANES), rank, 1).reshape(block, most, LANES)
    high = jnp.where(lax.broadcasted_iota(jnp.int32, (block, most, LANES), 2) < rank, 0.0, 1.0)
    for h in range(halves):
        wanted = named(names_ref, step, h, block, most)
        chosen = jnp.where(high == 1.0 * h, both, swapped)
        place = (wanted - high) * 0.5
        for c in range(held // LANES):
            value = jnp.where(place == 1.0 * c, chosen, 0.0)
            wide_ref[h, :, :, c * LANES : (c + 1) * LANES] = value.astype(BF16)
    wide = wide_ref[...].reshape(halves * block * most, held)
    out = jnp.dot(wide, up_ref[...], preferred_element_type=F32)
    out_ref[...] = out.astype(BF16).reshape(out_ref.shape)


def expand_rows(step, names, parts, up, rank, block=8):
    half, most, _ = parts[0].shape
    tiles = names.shape[1] - 1
    held, features = up.shape
    names = names.reshape((2, half) + names.shape[1:])
    delta = pl.pallas_call(
        functools.partial(expand_kernel, step, rank),
        out_shape=pltpu.HBM((2, half, most, features), BF16),
        grid=(half // block,),
        in_specs=[pl.BlockSpec((2, block, 1, TILE, LANES), lambda i: (0, i, tiles, 0, 0))]
        + [pl.BlockSpec((block, most, LANES), lambda i: (i, 0, 0))] * len(parts)
        + [pl.BlockSpec((held, features), lambda i: (0, 0))],
        out_specs=pl.BlockSpec((2, block, most, features), lambda i: (0, i, 0, 0)),
        scratch_shapes=[pltpu.VMEM((2, block, most, held), BF16)],
        compiler_params=pltpu.CompilerParams(vmem_limit_bytes=VMEM),
        cost_estimate=pl.CostEstimate(
            flops=4 * half * most * held * features,
            bytes_accessed=2 * (5 * half * most * LANES + up.size + 2 * half * most * features),
            transcendentals=0,
        ),
        name="expand",
    )(names, *parts, up)
    return delta.reshape(2 * half, most, features)


def shares_kernel(order_ref, tokens_ref, weight_ref, out_ref):
    out_ref[0] = jnp.dot(tokens_ref[...], weight_ref[...], preferred_element_type=F32)


def base_shares(flat_tokens, query_weight, distances):
    size = lax.axis_size("tp")
    rows, width = flat_tokens.shape
    columns = query_weight.shape[1] // size
    order = lax.rem(lax.axis_index("tp") + jnp.array(distances, jnp.int32), size)
    amount = len(distances)
    return pl.pallas_call(
        shares_kernel,
        out_shape=jax.ShapeDtypeStruct((amount, rows, columns), F32),
        grid_spec=pltpu.PrefetchScalarGridSpec(
            num_scalar_prefetch=1,
            grid=(amount,),
            in_specs=[
                pl.BlockSpec((rows, width), lambda k, order: (0, 0)),
                pl.BlockSpec((width, columns), lambda k, order: (0, order[k])),
            ],
            out_specs=pl.BlockSpec((1, rows, columns), lambda k, order: (k, 0, 0)),
        ),
        compiler_params=pltpu.CompilerParams(vmem_limit_bytes=VMEM),
        cost_estimate=pl.CostEstimate(
            flops=2 * rows * width * columns * amount,
            bytes_accessed=2 * width * columns * amount + 4 * rows * columns * amount,
            transcendentals=0,
        ),
        name="shares",
    )(order, flat_tokens, query_weight)


def first_sums_kernel(shares_ref, top_ref, low_ref, right_ref, left_ref):
    middle = top_ref.shape[0]
    right_ref[:middle] = (shares_ref[0, :middle] + top_ref[...].astype(F32)).astype(BF16)
    right_ref[middle:] = shares_ref[0, middle:].astype(BF16)
    left_ref[:middle] = shares_ref[1, :middle].astype(BF16)
    left_ref[middle:] = (shares_ref[1, middle:] + low_ref[...].astype(F32)).astype(BF16)


def first_sums(shares, top, low):
    _, rows, columns = shares.shape
    out = jax.ShapeDtypeStruct((rows, columns), BF16)
    return pl.pallas_call(
        first_sums_kernel,
        out_shape=(out, out),
        compiler_params=pltpu.CompilerParams(vmem_limit_bytes=VMEM),
        cost_estimate=pl.CostEstimate(
            flops=2 * rows * columns, bytes_accessed=14 * rows * columns, transcendentals=0
        ),
        name="first_sums",
    )(shares, top, low)


def join_kernel(spread_ref, back_ref, base_ref, earlier_ref, out_ref):
    groups, most, features = back_ref.shape
    back = back_ref[...].reshape(groups * most, features)
    delta = jnp.dot(spread_ref[...], back, preferred_element_type=F32)
    out_ref[0] = (base_ref[...] + delta).astype(BF16)


def join(step, spread, back, base, earlier):
    rows, places = spread.shape
    groups, most, features = back.shape
    return pl.pallas_call(
        join_kernel,
        out_shape=jax.ShapeDtypeStruct(earlier.shape, BF16),
        grid=(1,),
        in_specs=[
            pl.BlockSpec((rows, places), lambda i: (0, 0)),
            pl.BlockSpec((groups, most, features), lambda i: (0, 0, 0)),
            pl.BlockSpec((rows, features), lambda i: (0, 0)),
            pl.BlockSpec(memory_space=pl.ANY),
        ],
        out_specs=pl.BlockSpec((1, rows, features), lambda i: (step, 0, 0)),
        input_output_aliases={3: 0},
        compiler_params=pltpu.CompilerParams(vmem_limit_bytes=VMEM),
        cost_estimate=pl.CostEstimate(
            flops=2 * rows * places * features,
            bytes_accessed=2 * (spread.size + back.size) + 6 * base.size,
            transcendentals=0,
        ),
        name="join",
    )(spread, back, base, earlier)


def parts_over_tp(value, early):
    size = lax.axis_size("tp")
    assert size == 8

    def fetch(value, ahead):
        return lax.ppermute(value, "tp", [((i + ahead) % size, i) for i in range(size)])

    after, before = fetch(value, 1), fetch(value, -1)
    two = (value.astype(F32) + after.astype(F32)).astype(BF16)
    if early:
        value, after, two = lax.optimization_barrier((value, after, two))
    three = value.astype(F32) + after.astype(F32) + before.astype(F32)
    return value, after, before, fetch(three.astype(BF16), 3), fetch(two, -3)


def body(tokens, query_weight, down_weight, up_weight, requests, row_slot_index):
    count = lax.axis_size("pool")
    size = lax.axis_size("tp")
    steps, rows, width = tokens.shape
    most = 4 * rows // count
    adapters, rank, _ = down_weight.shape
    features = up_weight.shape[-1]
    middle = steps * rows // 2
    right = [(i, (i + 1) % size) for i in range(size)]
    left = [(i, (i - 1) % size) for i in range(size)]

    def swap(value):
        return lax.all_to_all(value, "pool", split_axis=0, concat_axis=0, tiled=True)

    asked = requests[:, 0, :]
    sent = pack(0, asked, row_slot_index, tokens, most)
    sent, late_tokens, late_slots = lax.optimization_barrier((sent, tokens, row_slot_index))
    x = [swap(sent)]
    sent = pack(1, asked, late_slots, late_tokens, most)

    late_tokens = late_tokens.reshape(steps * rows, width)
    far = size // 2
    far_weight = pltpu.with_memory_space_constraint(query_weight, pltpu.HBM)
    farthest = base_shares(late_tokens, far_weight, [far])[0].astype(BF16)
    top = lax.ppermute(farthest[:middle], "tp", right)
    low = lax.ppermute(farthest[middle:], "tp", left)
    late_tokens, _ = lax.optimization_barrier((late_tokens, farthest))
    near = [d for ahead in range(far - 2, 0, -1) for d in (ahead, size - ahead)] + [0]
    first = base_shares(late_tokens, query_weight, [far - 1, far + 1])
    late_tokens, first = lax.optimization_barrier((late_tokens, first))
    going_right, going_left = first_sums(first, top, low)
    late_tokens, _ = lax.optimization_barrier((late_tokens, going_right))
    shares = base_shares(late_tokens, query_weight, near)
    down = pltpu.with_memory_space_constraint(down_weight.reshape(adapters * rank, width), pltpu.HBM)
    going_right = lax.ppermute(going_right, "tp", right)
    going_left = lax.ppermute(going_left, "tp", left)
    names = x[0]
    shrunk = shrink_rows(0, names, x[0], down, most, rank)
    sent, going_right, going_left, shares = lax.optimization_barrier((sent, going_right, going_left, shares))
    x.append(swap(sent))
    going_right = (going_right.astype(F32) + shares[0]).astype(BF16)
    going_left = (going_left.astype(F32) + shares[1]).astype(BF16)

    up = up_weight.reshape(adapters * rank, features)
    back = []
    delta = expand_rows(0, names, parts_over_tp(shrunk, True), up, rank)
    going_right = lax.ppermute(going_right, "tp", right)
    going_left = lax.ppermute(going_left, "tp", left)
    shrunk = shrink_rows(1, names, x[1], down, most, rank)
    delta, shrunk = lax.optimization_barrier((delta, shrunk))
    back.append(swap(delta))
    delta = expand_rows(1, names, parts_over_tp(shrunk, False), up, rank)
    going_right = (going_right.astype(F32) + shares[2]).astype(BF16)
    going_left = (going_left.astype(F32) + shares[3]).astype(BF16)
    delta, going_right, going_left = lax.optimization_barrier((delta, going_right, going_left))
    back.append(swap(delta))
    from_left = lax.ppermute(going_right, "tp", right).astype(F32)
    from_right = lax.ppermute(going_left, "tp", left).astype(F32)
    base = (shares[-1] + from_left + from_right).reshape(steps, rows, features)

    slots = late_slots[:, 0, :]
    before = slots[:, None, :] < jnp.arange(count, dtype=jnp.int32)[None, :, None]
    start = jnp.minimum(jnp.sum(before.astype(jnp.int32), axis=2), rows - most)
    mine = slots[:, :, None] == jnp.arange(count, dtype=jnp.int32)[None, None, :]
    own_start = jnp.sum(jnp.where(mine, start[:, None, :], 0), axis=2)
    place = slots * most + jnp.arange(rows, dtype=jnp.int32)[None, :] - own_start
    spread = (place[:, :, None] == jnp.arange(count * most, dtype=jnp.int32)[None, None, :]).astype(BF16)
    out = jnp.zeros((steps, rows, features), BF16)
    for t in range(steps):
        out = join(t, spread[t], back[t], base[t], out)
    return out


def solution(mesh):
    placed = (
        P(None, "pool", "tp"),
        P("tp", None),
        P("pool", None, "tp"),
        P("pool", None, "tp"),
        P(None, "pool", None),
        P(None, "pool", None),
    )
    return jax.shard_map(
        body, mesh=mesh, in_specs=placed, out_specs=P(None, "pool", "tp"), check_vma=False
    )
```

```python
import functools

import jax
import jax.numpy as jnp
from jax import lax
from jax.experimental import pallas as pl
from jax.experimental.pallas import tpu as pltpu
from jax.sharding import PartitionSpec as P

BF16 = jnp.bfloat16
F32 = jnp.float32
LANES = 128
TILE = 16
VMEM = 26 << 20
FULL = 62 << 20


def pack_kernel(step, asked_ref, slots_ref, tokens_ref, out_ref):
    rows, width = tokens_ref.shape[1:]
    block = out_ref.shape[0]
    across = width // LANES
    most = out_ref.shape[1] // across * TILE
    first = pl.program_id(0) * block
    shape = (block, most, rows)
    slot = lax.broadcasted_iota(jnp.int32, shape, 0) + first
    ahead = lax.broadcasted_iota(jnp.int32, shape, 1)
    position = lax.broadcasted_iota(jnp.int32, shape, 2)
    held = jnp.broadcast_to(slots_ref[0].reshape(1, 1, rows), shape)
    before = jnp.where(held < slot, 1.0, 0.0)
    start = jnp.minimum(jnp.sum(before, axis=2, keepdims=True).astype(jnp.int32), rows - most)
    pick = jnp.where(position == start + ahead, 1.0, 0.0).astype(BF16)
    value = jnp.dot(pick.reshape(block * most, rows), tokens_ref[0], preferred_element_type=F32)
    value = value.astype(BF16).reshape(block, most // TILE, TILE, width)
    for down in range(most // TILE):
        for c in range(across):
            out_ref[:, down * across + c] = value[:, down, :, c * LANES : (c + 1) * LANES]
    if step == 0:
        shape = (block, TILE, asked_ref.shape[1])
        here = lax.broadcasted_iota(jnp.int32, shape, 2) == lax.broadcasted_iota(jnp.int32, shape, 0) + first
        line = lax.broadcasted_iota(jnp.int32, shape, 1)
        asked = jnp.where(
            line < TILE // 2,
            jnp.broadcast_to(asked_ref[0:1, :].reshape(1, 1, -1), shape),
            jnp.broadcast_to(asked_ref[1:2, :].reshape(1, 1, -1), shape),
        )
        names = jnp.sum(jnp.where(here, asked.astype(F32), 0.0), axis=2, keepdims=True)
        names = jnp.broadcast_to(names, (block, TILE, LANES))
        out_ref[:, most // TILE * across] = names.astype(BF16)


def pack(step, asked, slots, tokens, most, block=16):
    _, rows, width = tokens.shape
    count = asked.shape[1]
    tiles = (most // TILE) * (width // LANES) + (1 if step == 0 else 0)
    return pl.pallas_call(
        functools.partial(pack_kernel, step),
        out_shape=jax.ShapeDtypeStruct((count, tiles, TILE, LANES), BF16),
        grid=(count // block,),
        in_specs=[
            pl.BlockSpec(asked.shape, lambda i: (0, 0)),
            pl.BlockSpec((1, 1, rows), lambda i: (step, 0, 0)),
            pl.BlockSpec((1, rows, width), lambda i: (step, 0, 0)),
        ],
        out_specs=pl.BlockSpec((block, tiles, TILE, LANES), lambda i: (i, 0, 0, 0)),
        compiler_params=pltpu.CompilerParams(vmem_limit_bytes=FULL if step == 0 else VMEM),
        cost_estimate=pl.CostEstimate(
            flops=2 * count * most * rows * width,
            bytes_accessed=2 * (rows * width + count * tiles * TILE * LANES),
            transcendentals=0,
        ),
        name="pack",
    )(asked, slots, tokens)


def named(names_ref, step, half, block, most):
    line = step * (TILE // 2)
    return jnp.broadcast_to(
        names_ref[half, :, 0].astype(F32)[:, line : line + 1, :], (block, most, LANES)
    )


def shrink_kernel(step, rank, names_ref, x_ref, down_ref, out_ref, rows_ref, acc_ref):
    halves, block, most, held = acc_ref.shape
    width = rows_ref.shape[-1]
    across = width // LANES
    for d in range(rows_ref.shape[2]):
        for c in range(across):
            rows_ref[:, :, d, :, c * LANES : (c + 1) * LANES] = x_ref[:, :, d * across + c]
    acc = lax.dot_general(
        rows_ref[...].reshape(halves * block * most, width),
        down_ref[...],
        (((1,), (1,)), ((), ())),
        preferred_element_type=F32,
    )
    acc_ref[...] = acc.reshape(acc_ref.shape)
    lane = lax.broadcasted_iota(jnp.int32, (block * most, LANES), 1)
    parts = []
    for h in range(halves):
        wanted = named(names_ref, step, h, block, most)
        pair = jnp.floor(wanted * 0.5)
        odd = wanted - 2.0 * pair
        value = acc_ref[h, :, :, :LANES]
        for c in range(1, held // LANES):
            value = jnp.where(pair == 1.0 * c, acc_ref[h, :, :, c * LANES : (c + 1) * LANES], value)
        value = value.reshape(block * most, LANES)
        odd = odd.reshape(block * most, LANES)
        parts.append(jnp.where(odd == 1.0 * h, value, pltpu.roll(value, rank, 1)))
    out = jnp.where(lane < rank, parts[0], parts[1])
    out_ref[...] = out.astype(BF16).reshape(out_ref.shape)


def shrink_rows(step, names, x, down, most, rank, block=16):
    half = x.shape[0] // 2
    held, width = down.shape
    tiles = (most // TILE) * (width // LANES)
    names = names.reshape((2, half) + names.shape[1:])
    x = x.reshape((2, half) + x.shape[1:])
    return pl.pallas_call(
        functools.partial(shrink_kernel, step, rank),
        out_shape=jax.ShapeDtypeStruct((half, most, LANES), BF16),
        grid=(half // block,),
        in_specs=[
            pl.BlockSpec((2, block, 1, TILE, LANES), lambda i: (0, i, tiles, 0, 0)),
            pl.BlockSpec((2, block, tiles, TILE, LANES), lambda i: (0, i, 0, 0, 0)),
            pl.BlockSpec((held, width), lambda i: (0, 0)),
        ],
        out_specs=pl.BlockSpec((block, most, LANES), lambda i: (i, 0, 0)),
        scratch_shapes=[
            pltpu.VMEM((2, block, most // TILE, TILE, width), BF16),
            pltpu.VMEM((2, block, most, held), F32),
        ],
        compiler_params=pltpu.CompilerParams(vmem_limit_bytes=VMEM),
        cost_estimate=pl.CostEstimate(
            flops=4 * half * most * width * held,
            bytes_accessed=2 * (x.size + down.size),
            transcendentals=0,
        ),
        name="shrink",
    )(names, x, down)


def expand_kernel(step, rank, names_ref, a_ref, b_ref, c_ref, d_ref, e_ref, up_ref, out_ref, wide_ref):
    halves, block, most, held = wide_ref.shape
    both = a_ref[...].astype(F32)
    for ref in (b_ref, c_ref, d_ref, e_ref):
        both = both + ref[...].astype(F32)
    swapped = pltpu.roll(both.reshape(block * most, LANES), rank, 1).reshape(block, most, LANES)
    high = jnp.where(lax.broadcasted_iota(jnp.int32, (block, most, LANES), 2) < rank, 0.0, 1.0)
    for h in range(halves):
        wanted = named(names_ref, step, h, block, most)
        chosen = jnp.where(high == 1.0 * h, both, swapped)
        place = (wanted - high) * 0.5
        for c in range(held // LANES):
            value = jnp.where(place == 1.0 * c, chosen, 0.0)
            wide_ref[h, :, :, c * LANES : (c + 1) * LANES] = value.astype(BF16)
    wide = wide_ref[...].reshape(halves * block * most, held)
    out = jnp.dot(wide, up_ref[...], preferred_element_type=F32)
    out_ref[...] = out.astype(BF16).reshape(out_ref.shape)


def expand_rows(step, names, parts, up, rank, block=16):
    half, most, _ = parts[0].shape
    tiles = names.shape[1] - 1
    held, features = up.shape
    names = names.reshape((2, half) + names.shape[1:])
    delta = pl.pallas_call(
        functools.partial(expand_kernel, step, rank),
        out_shape=pltpu.HBM((2, half, most, features), BF16),
        grid=(half // block,),
        in_specs=[pl.BlockSpec((2, block, 1, TILE, LANES), lambda i: (0, i, tiles, 0, 0))]
        + [pl.BlockSpec((block, most, LANES), lambda i: (i, 0, 0))] * len(parts)
        + [pl.BlockSpec((held, features), lambda i: (0, 0))],
        out_specs=pl.BlockSpec((2, block, most, features), lambda i: (0, i, 0, 0)),
        scratch_shapes=[pltpu.VMEM((2, block, most, held), BF16)],
        compiler_params=pltpu.CompilerParams(vmem_limit_bytes=VMEM),
        cost_estimate=pl.CostEstimate(
            flops=4 * half * most * held * features,
            bytes_accessed=2 * (5 * half * most * LANES + up.size + 2 * half * most * features),
            transcendentals=0,
        ),
        name="expand",
    )(names, *parts, up)
    return delta.reshape(2 * half, most, features)


def shares_kernel(order_ref, tokens_ref, weight_ref, out_ref):
    out_ref[0] = jnp.dot(tokens_ref[...], weight_ref[...], preferred_element_type=F32)


def base_shares(flat_tokens, query_weight, distances):
    size = lax.axis_size("tp")
    rows, width = flat_tokens.shape
    columns = query_weight.shape[1] // size
    order = lax.rem(lax.axis_index("tp") + jnp.array(distances, jnp.int32), size)
    amount = len(distances)
    return pl.pallas_call(
        shares_kernel,
        out_shape=jax.ShapeDtypeStruct((amount, rows, columns), F32),
        grid_spec=pltpu.PrefetchScalarGridSpec(
            num_scalar_prefetch=1,
            grid=(amount,),
            in_specs=[
                pl.BlockSpec((rows, width), lambda k, order: (0, 0)),
                pl.BlockSpec((width, columns), lambda k, order: (0, order[k])),
            ],
            out_specs=pl.BlockSpec((1, rows, columns), lambda k, order: (k, 0, 0)),
        ),
        compiler_params=pltpu.CompilerParams(vmem_limit_bytes=VMEM),
        cost_estimate=pl.CostEstimate(
            flops=2 * rows * width * columns * amount,
            bytes_accessed=2 * width * columns * amount + 4 * rows * columns * amount,
            transcendentals=0,
        ),
        name="shares",
    )(order, flat_tokens, query_weight)


def first_sums_kernel(shares_ref, top_ref, low_ref, right_ref, left_ref):
    middle = top_ref.shape[0]
    right_ref[:middle] = (shares_ref[0, :middle] + top_ref[...].astype(F32)).astype(BF16)
    right_ref[middle:] = shares_ref[0, middle:].astype(BF16)
    left_ref[:middle] = shares_ref[1, :middle].astype(BF16)
    left_ref[middle:] = (shares_ref[1, middle:] + low_ref[...].astype(F32)).astype(BF16)


def first_sums(shares, top, low):
    _, rows, columns = shares.shape
    out = jax.ShapeDtypeStruct((rows, columns), BF16)
    return pl.pallas_call(
        first_sums_kernel,
        out_shape=(out, out),
        compiler_params=pltpu.CompilerParams(vmem_limit_bytes=VMEM),
        cost_estimate=pl.CostEstimate(
            flops=2 * rows * columns, bytes_accessed=14 * rows * columns, transcendentals=0
        ),
        name="first_sums",
    )(shares, top, low)


def join_kernel(spread_ref, back_ref, base_ref, earlier_ref, out_ref):
    groups, most, features = back_ref.shape
    back = back_ref[...].reshape(groups * most, features)
    delta = jnp.dot(spread_ref[...], back, preferred_element_type=F32)
    out_ref[0] = (base_ref[...] + delta).astype(BF16)


def join(step, spread, back, base, earlier):
    rows, places = spread.shape
    groups, most, features = back.shape
    return pl.pallas_call(
        join_kernel,
        out_shape=jax.ShapeDtypeStruct(earlier.shape, BF16),
        grid=(1,),
        in_specs=[
            pl.BlockSpec((rows, places), lambda i: (0, 0)),
            pl.BlockSpec((groups, most, features), lambda i: (0, 0, 0)),
            pl.BlockSpec((rows, features), lambda i: (0, 0)),
            pl.BlockSpec(memory_space=pl.ANY),
        ],
        out_specs=pl.BlockSpec((1, rows, features), lambda i: (step, 0, 0)),
        input_output_aliases={3: 0},
        compiler_params=pltpu.CompilerParams(vmem_limit_bytes=VMEM),
        cost_estimate=pl.CostEstimate(
            flops=2 * rows * places * features,
            bytes_accessed=2 * (spread.size + back.size) + 6 * base.size,
            transcendentals=0,
        ),
        name="join",
    )(spread, back, base, earlier)


def parts_over_tp(value, early):
    size = lax.axis_size("tp")
    assert size == 8

    def fetch(value, ahead):
        return lax.ppermute(value, "tp", [((i + ahead) % size, i) for i in range(size)])

    after, before = fetch(value, 1), fetch(value, -1)
    two = (value.astype(F32) + after.astype(F32)).astype(BF16)
    if early:
        value, after, two = lax.optimization_barrier((value, after, two))
    three = value.astype(F32) + after.astype(F32) + before.astype(F32)
    return value, after, before, fetch(three.astype(BF16), 3), fetch(two, -3)


def body(tokens, query_weight, down_weight, up_weight, requests, row_slot_index):
    count = lax.axis_size("pool")
    size = lax.axis_size("tp")
    steps, rows, width = tokens.shape
    most = 4 * rows // count
    adapters, rank, _ = down_weight.shape
    features = up_weight.shape[-1]
    middle = steps * rows // 2
    right = [(i, (i + 1) % size) for i in range(size)]
    left = [(i, (i - 1) % size) for i in range(size)]

    def swap(value):
        return lax.all_to_all(value, "pool", split_axis=0, concat_axis=0, tiled=True)

    asked = requests[:, 0, :]
    sent = pack(0, asked, row_slot_index, tokens, most)
    sent, late_tokens, late_slots = lax.optimization_barrier((sent, tokens, row_slot_index))
    x = [swap(sent)]
    sent = pack(1, asked, late_slots, late_tokens, most)

    late_tokens = late_tokens.reshape(steps * rows, width)
    far = size // 2
    far_weight = pltpu.with_memory_space_constraint(query_weight, pltpu.HBM)
    farthest = base_shares(late_tokens, far_weight, [far])[0].astype(BF16)
    top = lax.ppermute(farthest[:middle], "tp", right)
    low = lax.ppermute(farthest[middle:], "tp", left)
    late_tokens, _ = lax.optimization_barrier((late_tokens, farthest))
    near = [d for ahead in range(far - 2, 0, -1) for d in (ahead, size - ahead)] + [0]
    first = base_shares(late_tokens, query_weight, [far - 1, far + 1])
    late_tokens, first = lax.optimization_barrier((late_tokens, first))
    going_right, going_left = first_sums(first, top, low)
    late_tokens, _ = lax.optimization_barrier((late_tokens, going_right))
    shares = base_shares(late_tokens, query_weight, near)
    down = pltpu.with_memory_space_constraint(down_weight.reshape(adapters * rank, width), pltpu.HBM)
    going_right = lax.ppermute(going_right, "tp", right)
    going_left = lax.ppermute(going_left, "tp", left)
    names = x[0]
    shrunk = shrink_rows(0, names, x[0], down, most, rank)
    sent, going_right, going_left, shares = lax.optimization_barrier((sent, going_right, going_left, shares))
    x.append(swap(sent))
    going_right = (going_right.astype(F32) + shares[0]).astype(BF16)
    going_left = (going_left.astype(F32) + shares[1]).astype(BF16)

    up = up_weight.reshape(adapters * rank, features)
    back = []
    delta = expand_rows(0, names, parts_over_tp(shrunk, True), up, rank)
    going_right = lax.ppermute(going_right, "tp", right)
    going_left = lax.ppermute(going_left, "tp", left)
    shrunk = shrink_rows(1, names, x[1], down, most, rank)
    delta, shrunk = lax.optimization_barrier((delta, shrunk))
    back.append(swap(delta))
    delta = expand_rows(1, names, parts_over_tp(shrunk, False), up, rank)
    going_right = (going_right.astype(F32) + shares[2]).astype(BF16)
    going_left = (going_left.astype(F32) + shares[3]).astype(BF16)
    delta, going_right, going_left = lax.optimization_barrier((delta, going_right, going_left))
    back.append(swap(delta))
    from_left = lax.ppermute(going_right, "tp", right).astype(F32)
    from_right = lax.ppermute(going_left, "tp", left).astype(F32)
    base = (shares[-1] + from_left + from_right).reshape(steps, rows, features)

    slots = late_slots[:, 0, :]
    before = slots[:, None, :] < jnp.arange(count, dtype=jnp.int32)[None, :, None]
    start = jnp.minimum(jnp.sum(before.astype(jnp.int32), axis=2), rows - most)
    mine = slots[:, :, None] == jnp.arange(count, dtype=jnp.int32)[None, None, :]
    own_start = jnp.sum(jnp.where(mine, start[:, None, :], 0), axis=2)
    place = slots * most + jnp.arange(rows, dtype=jnp.int32)[None, :] - own_start
    spread = (place[:, :, None] == jnp.arange(count * most, dtype=jnp.int32)[None, None, :]).astype(BF16)
    out = jnp.zeros((steps, rows, features), BF16)
    for t in range(steps):
        out = join(t, spread[t], back[t], base[t], out)
    return out


def solution(mesh):
    placed = (
        P(None, "pool", "tp"),
        P("tp", None),
        P("pool", None, "tp"),
        P("pool", None, "tp"),
        P(None, "pool", None),
        P(None, "pool", None),
    )
    return jax.shard_map(
        body, mesh=mesh, in_specs=placed, out_specs=P(None, "pool", "tp"), check_vma=False
    )
```
